128 devices in a mesh: lon: 32 (over z, x, core), lat: 4 (over y).
Axes of the slice: x: 4, y: 4, z: 4, core: 2. Of those that a mesh axis runs over, the one named last changes fastest.
Arguments:
- absorber: bfloat16 [256, 90, 4096], P('lat', None, 'lon'), may hold values from 0.049804688 to 1
- cos_zenith: bfloat16 [256, 4096], P('lat', 'lon'), may hold values from 0.099609375 to 1
- albedo: bfloat16 [256, 4096], P('lat', 'lon'), may hold values from 0.049804688 to 0.796875
- absorption: float32 [16, 90], replicated, may hold values from 0.002 to 0.05
- gpoint_weight: float32 [16], replicated, may hold values from 0.02 to 0.12
- sunlit: int32 [256, 32], P('lat', 'lon'), may hold values from 0 to 1, as said below
- area_weight: float32 [256, 4096], P('lat', 'lon'), may hold values from 0.1 to 1
- land_owner: int32 [256, 32], P('lat', 'lon'), may hold values from 0 to 127, as said below
- land_block: int32 [256, 32], P('lat', 'lon'), may hold values from 0 to 15
- land_cell: int32 [256, 4096], P('lat', 'lon'), may hold values from 0 to 127
- soil_temp: float32 [12, 2048, 128], P(None, ('lon', 'lat')), may hold values from -6 to 6
- heat_capacity: float32 [12, 2048, 128], P(None, ('lon', 'lat')), may hold values from 0.5 to 2
- conductance: float32 [12, 2048, 128], P(None, ('lon', 'lat')), may hold values from 0.3 to 3
Outputs:
- heating: float32 [256, 90, 4096], P('lat', None, 'lon')
- soil_next: float32 [12, 2048, 128], P(None, ('lon', 'lat'))
The draws below stay inside these ranges and needn't reach their ends.
Inputs may be any that keep to these rules, and one draw needn't show every extreme that they name: Of the same row of blocks on two devices 32/2 apart along lon, exactly one is sunlit; in each latitude band the day side covers a contiguous half of the cycle. `land_owner`: the 64 blocks of one device name each owner exactly 1 times when 64 is at least the device count, else at most once.
All inputs are finite; a program needn't handle non-finite values.
Results may differ from the reference program's by a relative error of at most 0.00045.
Values may be sent and summed in bfloat16 or wider, within the bound.
No kernel may reach another device: no remote copies, remote signals or barrier semaphores. Data moves between devices by JAX's collectives and lax.ppermute only.
A program may use at most 64 MiB of HBM per device.

```python
import math
import jax
import jax.numpy as jnp
from jax import lax

NB = 64
BC = 128
LEV = 90
G = 16
LC = 128
LANDB = 16
SOIL = 12
ROWS = 256
COLS = 4096
LANDALL = 2048
N_LON = 32
N_LAT = 4


def draw_sunlit(key, part):
    key = jax.random.fold_in(key, 11)
    first_key, second_key = jax.random.split(key)
    band_start = jax.random.randint(first_key, (N_LAT,), 0, N_LON)
    jitter_rows = jax.random.randint(second_key, (N_LAT, NB), 0, 3)
    row_start = (band_start[:, None] + jitter_rows) % N_LON
    longitude = jnp.arange(N_LON)
    lit_mask = (longitude[None, None, :] - row_start[:, :, None]) % N_LON < N_LON // 2
    return lit_mask.astype(jnp.int32).reshape(N_LAT * NB, N_LON)


def draw_land_owner(key, part):
    key = jax.random.fold_in(key, 23)
    devices_all = N_LON * N_LAT
    device_keys = jax.random.split(key, devices_all)
    orders = jax.vmap(lambda one_key: jax.random.permutation(one_key, devices_all))(device_keys)
    orders = orders.reshape(N_LAT, N_LON, devices_all)
    picks = jnp.arange(NB) % devices_all
    chosen = orders[:, :, picks]
    return jnp.transpose(chosen, (0, 2, 1)).reshape(N_LAT * NB, N_LON).astype(jnp.int32)


def set_ends(array, key, low, top_value):
    place = [jax.random.randint(jax.random.fold_in(key, axis), (), 0, length) for axis, length in enumerate(array.shape)]
    main_axis = array.shape.index(max(array.shape))
    beside = place[:main_axis] + [(place[main_axis] + 1) % array.shape[main_axis]] + place[main_axis + 1:]
    return array.at[tuple(place)].set(low).at[tuple(beside)].set(top_value)


def shard_levels(rng, extent, shards, least, largest):
    def one(axis_at, parts):
        draws = jax.random.uniform(jax.random.fold_in(jax.random.fold_in(rng, 6), axis_at), (parts,), jnp.float32, least / len(shards), largest / len(shards))
        return jnp.repeat(jnp.exp(draws), extent[axis_at] // parts).reshape((-1,) + (1,) * (len(extent) - axis_at - 1))

    gain = one(*shards[0])
    for cut in shards[1:]:
        gain = gain * one(*cut)
    return gain


def normal_values(key, dims, deviation, bound, shards=(), dtype=jnp.bfloat16):
    array = deviation * jax.random.normal(key, dims, jnp.float32)
    if shards:
        array = array * shard_levels(key, dims, shards, -0.22, 0.18)
    return jnp.clip(array, -bound, bound).astype(dtype)


def setup_inputs(seed: int = 0) -> dict:
    keys = jax.random.split(jax.random.key(seed), 14)
    absorber = jnp.clip(jnp.exp(math.log(1.0) - 2.9996462 * jax.random.uniform(keys[0], (ROWS, LEV, COLS), jnp.float32) ** shard_levels(keys[0], (ROWS, LEV, COLS), ((0, 4), (2, 32)), -0.2, 0.2)), 0.049804688, 1.0).astype(jnp.bfloat16)
    cos_zenith = jnp.clip(0.099609375 + 0.9003906 * jax.random.uniform(keys[1], (ROWS, COLS), jnp.float32) ** shard_levels(keys[1], (ROWS, COLS), ((0, 4), (1, 32)), -0.2, 0.2), 0.099609375, 1.0).astype(jnp.bfloat16)
    albedo = jnp.clip(0.049804688 + 0.7470703 * jax.random.uniform(keys[2], (ROWS, COLS), jnp.float32) ** shard_levels(keys[2], (ROWS, COLS), ((0, 4), (1, 32)), -0.2, 0.2), 0.049804688, 0.796875).astype(jnp.bfloat16)
    absorption = jnp.clip(jnp.exp(jax.random.uniform(keys[3], (G, LEV), jnp.float32, math.log(0.002), math.log(0.05))), 0.002, 0.05)
    gpoint_weight = jnp.clip(jnp.exp(jax.random.uniform(keys[4], (G,), jnp.float32, math.log(0.02), math.log(0.12))), 0.02, 0.12)
    sunlit = draw_sunlit(jax.random.fold_in(keys[13], 71), 0)
    area_weight = jnp.clip(0.1 + 0.9 * jax.random.uniform(keys[6], (ROWS, COLS), jnp.float32) ** shard_levels(keys[6], (ROWS, COLS), ((0, 4), (1, 32)), -0.2, 0.2), 0.1, 1.0)
    land_owner = draw_land_owner(jax.random.fold_in(keys[13], 71), 0)
    land_block = set_ends(jax.random.randint(keys[8], (ROWS, N_LON), 0, LANDB), jax.random.fold_in(keys[8], 1), 0, LANDB - 1).astype(jnp.int32)
    land_cell = set_ends(jax.random.randint(keys[9], (ROWS, COLS), 0, LC), jax.random.fold_in(keys[9], 1), 0, LC - 1).astype(jnp.int32)
    soil_temp = normal_values(keys[10], (SOIL, LANDALL, LC), 1.0, 6.0, ((1, 128),), jnp.float32)
    heat_capacity = jnp.clip(jnp.exp(math.log(2.0) - 1.3862944 * jax.random.uniform(keys[11], (SOIL, LANDALL, LC), jnp.float32) ** shard_levels(keys[11], (SOIL, LANDALL, LC), ((1, 128),), -0.2, 0.2)), 0.5, 2.0)
    conductance = jnp.clip(jnp.exp(math.log(3.0) - 2.3025851 * jax.random.uniform(keys[12], (SOIL, LANDALL, LC), jnp.float32) ** shard_levels(keys[12], (SOIL, LANDALL, LC), ((1, 128),), -0.2, 0.2)), 0.3, 3.0)
    return {"absorber": absorber, "cos_zenith": cos_zenith, "albedo": albedo, "absorption": absorption, "gpoint_weight": gpoint_weight, "sunlit": sunlit, "area_weight": area_weight, "land_owner": land_owner, "land_block": land_block, "land_cell": land_cell, "soil_temp": soil_temp, "heat_capacity": heat_capacity, "conductance": conductance}


diffusivity = 1.66


def radiate(absorber, cosine, albedo_f, absorption, gpoint_weight):
    block_count, levels, columns = absorber.shape
    path_f = absorber.astype(jnp.float32)
    inverse = 1.0 / cosine

    def gpoint_step(gpoint, state_pair):
        net_flux, surface = state_pair
        depth = absorption[gpoint][None, :, None] * path_f
        depth_above = jnp.concatenate([jnp.zeros((block_count, 1, columns), jnp.float32), jnp.cumsum(depth, axis=1)], axis=1)
        column_depth = depth_above[:, -1]
        down_flux = cosine[:, None, :] * jnp.exp(-depth_above * inverse[:, None, :])
        surface_down = down_flux[:, -1]
        up_flux = (albedo_f * surface_down)[:, None, :] * jnp.exp(-diffusivity * (column_depth[:, None, :] - depth_above))
        net_flux = net_flux + gpoint_weight[gpoint] * (down_flux - up_flux)
        surface = surface + gpoint_weight[gpoint] * (1.0 - albedo_f) * surface_down
        return net_flux, surface

    start_pair = (jnp.zeros((block_count, levels + 1, columns), jnp.float32), jnp.zeros((block_count, columns), jnp.float32))
    net_flux, surface = lax.fori_loop(0, absorption.shape[0], gpoint_step, start_pair)
    return net_flux[:, :-1] - net_flux[:, 1:], surface


def solve_soil(soil_temp, heat_capacity, conductance, land_flux):
    layers = soil_temp.shape[0]
    upper_ratio = []
    scaled_rhs = []
    for layer in range(layers):
        right_side = heat_capacity[layer] * soil_temp[layer]
        diagonal = heat_capacity[layer] + conductance[layer]
        if layer == 0:
            right_side = right_side + land_flux
            pivot_value = diagonal
            scaled = right_side / pivot_value
        else:
            diagonal = diagonal + conductance[layer - 1]
            pivot_value = diagonal + conductance[layer - 1] * upper_ratio[-1]
            scaled = (right_side + conductance[layer - 1] * scaled_rhs[-1]) / pivot_value
        upper_ratio.append(-conductance[layer] / pivot_value)
        scaled_rhs.append(scaled)
    solved = [scaled_rhs[-1]]
    for layer in range(layers - 2, -1, -1):
        solved.append(scaled_rhs[layer] - upper_ratio[layer] * solved[-1])
    return jnp.stack(solved[::-1], axis=0)


def reference(absorber, cos_zenith, albedo, absorption, gpoint_weight, sunlit, area_weight, land_owner, land_block, land_cell, soil_temp, heat_capacity, conductance):
    row_total, levels, columns = absorber.shape
    sun_mask = jnp.repeat(sunlit, BC, axis=1).astype(jnp.float32)
    cosine = cos_zenith.astype(jnp.float32)
    albedo_f = albedo.astype(jnp.float32)

    def band_pass(inputs):
        return radiate(inputs[0], inputs[1], inputs[2], absorption, gpoint_weight)

    heating, surface = lax.map(band_pass, (absorber.reshape(N_LAT, NB, levels, columns), cosine.reshape(N_LAT, NB, columns), albedo_f.reshape(N_LAT, NB, columns)))
    heating = heating.reshape(row_total, levels, columns) * sun_mask[:, None, :]
    surface = surface.reshape(row_total, columns) * sun_mask
    contrib = area_weight * surface
    owner_cols = jnp.repeat(land_owner, BC, axis=1).astype(jnp.int32)
    block_cols = jnp.repeat(land_block, BC, axis=1).astype(jnp.int32)
    target = (owner_cols * LANDB + block_cols) * LC + land_cell
    land_flux = jax.ops.segment_sum(contrib.reshape(-1), target.reshape(-1).astype(jnp.int32), num_segments=N_LON * N_LAT * LANDB * LC)
    land_flux = land_flux.reshape(N_LON * N_LAT * LANDB, LC)
    return heating, solve_soil(soil_temp, heat_capacity, conductance, land_flux)
```

```python
import functools
import math

import jax
import jax.numpy as jnp
from jax import lax
from jax.experimental import pallas as pl
from jax.experimental.pallas import tpu as pltpu
from jax.sharding import PartitionSpec as P

diffusivity = 1.66
log2e = math.log2(math.e)
f32 = jnp.float32
bf16 = jnp.bfloat16

LANES = 128
GP = 16
LEVELS = 90
KROWS = 96
CHUNKS = 12
STEP = 16


def high_part(x):
    return x.astype(bf16).astype(f32)


def coefficient_rows(absorption, weight_rows):
    scaled = absorption * (diffusivity * log2e)
    high = high_part(scaled)
    low = scaled - high
    offset = jnp.log2(weight_rows) * (-diffusivity)
    first = high_part(offset)
    second = high_part(offset - first)
    third = offset - first - second
    lane = lax.broadcasted_iota(jnp.int32, (GP, 6), 1)
    terms = jnp.where(
        lane == 0, first[:, :6], jnp.where(lane == 1, second[:, :6], jnp.where(lane == 2, third[:, :6], 0.0))
    )
    zeros = jnp.zeros((GP, 6), f32)
    tail = jnp.zeros((GP, 256 - 2 * KROWS), f32)
    return jnp.concatenate([high, terms, low, zeros, tail], axis=1)


def surface_kernel(
    sun, owner, target, weight, absorption, path, cosine, albedo, area, cell,
    rows_out, factor_out, coef_out, send_out,
    wide, weight_rows, coef, mu, nu, alb, contrib,
):
    step = pl.program_id(0)

    @pl.when(step == 0)
    def _():
        for g in range(GP):
            weight_rows[g : g + 1, :] = jnp.full((1, LANES), weight[g], f32)
        rows = coefficient_rows(absorption[...], weight_rows[...])
        coef_out[...] = rows
        coef[...] = rows.astype(bf16)
        send_out[...] = jnp.zeros(send_out.shape, f32)

    cos_f = cosine[...].astype(f32)
    mu[...] = cos_f
    nu[...] = (-1.0 / diffusivity) / cos_f
    alb[...] = albedo[...].astype(f32)
    wide[0 : LEVELS * STEP, :] = path[...].astype(f32).reshape(LEVELS * STEP, LANES)
    for extra in range(LEVELS, KROWS):
        wide[extra * STEP : (extra + 1) * STEP, :] = cos_f
    last = coef[:, : 2 * KROWS]
    for pair in range(STEP // 2):
        cols = []
        for half in range(2):
            block = 2 * pair + half
            rows = wide[pl.ds(block, KROWS, stride=STEP), :].astype(bf16)
            rows_out[block] = rows
            cols.append(rows)
        once = jnp.concatenate(cols, axis=1)
        depth = jnp.dot(last, jnp.concatenate([once, once], axis=0), preferred_element_type=f32)
        for half in range(2):
            block = 2 * pair + half
            part = depth[:, half * LANES : (half + 1) * LANES]
            nu_row = nu[block : block + 1, :]
            alb_row = alb[block : block + 1, :]
            factor_out[block] = alb_row * jnp.exp2(part * (nu_row - 1.0))
            total = jnp.sum(jnp.exp2(part * nu_row), axis=0, keepdims=True)
            flux = (1.0 - alb_row) * mu[block : block + 1, :] * total
            contrib[block : block + 1, :] = area[block : block + 1, :] * flux
    cell_ids = lax.broadcasted_iota(jnp.int32, (LANES, LANES), 0)
    row_ids = lax.broadcasted_iota(jnp.int32, (STEP, 2 * LANES), 0)
    lane_half = lax.broadcasted_iota(jnp.int32, (STEP, 2 * LANES), 1) // LANES
    for pair in range(STEP // 2):
        hots = []
        values = []
        for half in range(2):
            block = 2 * pair + half
            hots.append(jnp.where(cell[block : block + 1, :] == cell_ids, 1.0, 0.0).astype(bf16))
            values.append(jnp.broadcast_to(contrib[block : block + 1, :], (STEP, LANES)))
        value = jnp.concatenate(values, axis=1)
        first = high_part(value)
        second = high_part(value - first)
        third = value - first - second
        which = jnp.where(row_ids // 3 == lane_half, row_ids % 3, 3)
        left = jnp.where(which == 0, first, jnp.where(which == 1, second, jnp.where(which == 2, third, 0.0)))
        sums = lax.dot_general(
            left.astype(bf16),
            jnp.concatenate(hots, axis=1),
            (((1,), (1,)), ((), ())),
            preferred_element_type=f32,
        )
        for half in range(2):
            block = 2 * pair + half
            index = step * STEP + block
            row = sums[3 * half : 3 * half + 1] + sums[3 * half + 1 : 3 * half + 2] + sums[3 * half + 2 : 3 * half + 3]

            @pl.when(sun[0, index] == 1)
            def _():
                to = owner[0, index]
                send_out[to, 0:1, :] = row
                send_out[to, 1:2, :] = jnp.full((1, LANES), target[0, index].astype(f32))


def soil_ahead(temp, capacity, conduct, base_out, response_out):
    layers = temp.shape[0]
    ratio = []
    base = []
    response = []
    for layer in range(layers):
        right = capacity[layer] * temp[layer]
        diagonal = capacity[layer] + conduct[layer]
        if layer == 0:
            inverse = 1.0 / diagonal
            base.append(right * inverse)
            response.append(inverse)
        else:
            above = conduct[layer - 1]
            inverse = 1.0 / (diagonal + above + above * ratio[-1])
            base.append((right + above * base[-1]) * inverse)
            response.append(above * response[-1] * inverse)
        ratio.append(-conduct[layer] * inverse)
    x0 = base[-1]
    x1 = response[-1]
    base_out[layers - 1] = x0
    response_out[layers - 1] = x1
    for layer in range(layers - 2, -1, -1):
        x0 = base[layer] - ratio[layer] * x0
        x1 = response[layer] - ratio[layer] * x1
        base_out[layer] = x0
        response_out[layer] = x1


def radiate_kernel(
    sun, coef, rows, factor, cosine, temp, capacity, conduct,
    heat_out, base_out, response_out,
    weights, depth_a, depth_b, acc_a, acc_b, mu, nu,
):
    step = pl.program_id(0)

    @pl.when(step == 0)
    def _():
        lane = lax.broadcasted_iota(jnp.int32, (8, LANES), 1)
        row = lax.broadcasted_iota(jnp.int32, (8, LANES), 0)
        level_a = jnp.where(lane < LEVELS, lane, jnp.where(lane < KROWS, -1, lane - KROWS))
        level_b = lane + (LANES - KROWS)
        for chunk in range(CHUNKS):
            below_a = level_a < row + 8 * chunk
            below_b = level_b < row + 8 * chunk
            for g in range(0, GP, 2):
                at = (chunk * GP + g) * 8
                for tile, below in ((0, below_a), (1, below_b)):
                    lanes = slice(tile * LANES, (tile + 1) * LANES)
                    both = [jnp.where(below, coef[h : h + 1, lanes], 0.0) for h in (g, g + 1)]
                    weights[at : at + 16, lanes] = jnp.concatenate(both, axis=0).astype(bf16)
        soil_ahead(temp, capacity, conduct, base_out, response_out)

    cos_f = cosine[...].astype(f32)
    mu[...] = cos_f
    nu[...] = (-1.0 / diffusivity) / cos_f
    lit = sun[0, step * STEP]
    for block in range(1, STEP):
        lit = lit | sun[0, step * STEP + block]
    flat = heat_out.reshape(LEVELS * STEP, LANES)

    def depths(pair, depth):
        once = jnp.concatenate([rows[2 * pair], rows[2 * pair + 1]], axis=1)
        twice = jnp.concatenate([once, once], axis=0)
        for part in range(2):
            at = slice(part * 768, (part + 1) * 768)
            depth[at, :] = jnp.dot(weights[at, : 2 * KROWS], twice, preferred_element_type=f32)

    def fluxes(pair, depth, acc):
        for half in range(2):
            block = 2 * pair + half
            lanes = slice(half * LANES, (half + 1) * LANES)
            nu_rows = jnp.broadcast_to(nu[pl.ds(block, 1), :], (8, LANES))
            for chunk in range(CHUNKS):
                total = None
                for g in range(GP):
                    at = (chunk * GP + g) * 8
                    depth_now = depth[at : at + 8, lanes]
                    down = jnp.exp2(depth_now * nu_rows)
                    up = jnp.exp2(depth_now) * factor[block, g : g + 1, :]
                    total = down - up if total is None else (total + down) - up
                acc[chunk * 8 : chunk * 8 + 8, lanes] = total
            keep = (sun[0, step * STEP + block] == 1)
            scale = jnp.where(keep, mu[pl.ds(block, 1), :], 0.0)
            flat[pl.ds(block, LEVELS, stride=STEP), :] = (
                acc[0:LEVELS, lanes] - acc[1 : LEVELS + 1, lanes]
            ) * scale

    @pl.when(lit != 0)
    def _():
        depths(0, depth_a)

        def body(i, _):
            depths(2 * i + 1, depth_b)
            fluxes(2 * i, depth_a, acc_a)
            depths(jnp.minimum(2 * i + 2, STEP // 2 - 1), depth_a)
            fluxes(2 * i + 1, depth_b, acc_b)
            return 0

        lax.fori_loop(0, STEP // 4, body, 0)

    @pl.when(lit == 0)
    def _():
        heat_out[...] = jnp.zeros(heat_out.shape, f32)


def finish_kernel(got, base, response, soil_out):
    ids = got[:, 1, :]
    values = got[:, 0, :]
    sums = []
    for block in range(soil_out.shape[1]):
        sums.append(jnp.sum(jnp.where(ids == float(block), values, 0.0), axis=0, keepdims=True))
    flux = jnp.concatenate(sums, axis=0)
    soil_out[...] = base[...] + response[...] * flux[None]


def whole(shape):
    return pl.BlockSpec(shape, lambda i: (0,) * len(shape))


def surface_call(sun, owner, target, weight, absorption, path, cosine, albedo, area, cell, devices):
    blocks = path.shape[1]
    smem = pl.BlockSpec(memory_space=pltpu.SMEM)
    by_block = pl.BlockSpec((STEP, LANES), lambda i: (i, 0))
    return pl.pallas_call(
        surface_kernel,
        grid=(blocks // STEP,),
        in_specs=[
            smem, smem, smem, smem,
            whole((GP, LEVELS)),
            pl.BlockSpec((LEVELS, STEP, LANES), lambda i: (0, i, 0)),
            by_block, by_block, by_block, by_block,
        ],
        out_specs=[
            pl.BlockSpec((STEP, KROWS, LANES), lambda i: (i, 0, 0)),
            pl.BlockSpec((STEP, GP, LANES), lambda i: (i, 0, 0)),
            whole((GP, 256)),
            whole((devices, 2, LANES)),
        ],
        out_shape=[
            jax.ShapeDtypeStruct((blocks, KROWS, LANES), bf16),
            jax.ShapeDtypeStruct((blocks, GP, LANES), f32),
            jax.ShapeDtypeStruct((GP, 256), f32),
            jax.ShapeDtypeStruct((devices, 2, LANES), f32),
        ],
        scratch_shapes=[
            pltpu.VMEM((KROWS * STEP, LANES), f32),
            pltpu.VMEM((GP, LANES), f32),
            pltpu.VMEM((GP, 256), bf16),
            pltpu.VMEM((STEP, LANES), f32),
            pltpu.VMEM((STEP, LANES), f32),
            pltpu.VMEM((STEP, LANES), f32),
            pltpu.VMEM((STEP, LANES), f32),
        ],
        compiler_params=pltpu.CompilerParams(vmem_limit_bytes=24 * 1024 * 1024),
        cost_estimate=pl.CostEstimate(flops=10**9, bytes_accessed=4 * 10**6, transcendentals=10**6),
        name="surface",
    )(sun, owner, target, weight, absorption, path, cosine, albedo, area, cell)


def radiate_call(sun, coef, rows, factor, cosine, temp, capacity, conduct):
    blocks = rows.shape[0]
    soil = temp.shape
    return pl.pallas_call(
        radiate_kernel,
        grid=(blocks // STEP,),
        in_specs=[
            pl.BlockSpec(memory_space=pltpu.SMEM),
            whole((GP, 256)),
            pl.BlockSpec((STEP, KROWS, LANES), lambda i: (i, 0, 0)),
            pl.BlockSpec((STEP, GP, LANES), lambda i: (i, 0, 0)),
            pl.BlockSpec((STEP, LANES), lambda i: (i, 0)),
            whole(soil), whole(soil), whole(soil),
        ],
        out_specs=[
            pl.BlockSpec((LEVELS, STEP, LANES), lambda i: (0, i, 0)),
            whole(soil), whole(soil),
        ],
        out_shape=[
            jax.ShapeDtypeStruct((LEVELS, blocks, LANES), f32),
            jax.ShapeDtypeStruct(soil, f32),
            jax.ShapeDtypeStruct(soil, f32),
        ],
        scratch_shapes=[
            pltpu.VMEM((CHUNKS * GP * 8, 256), bf16),
            pltpu.VMEM((CHUNKS * GP * 8, 256), f32),
            pltpu.VMEM((CHUNKS * GP * 8, 256), f32),
            pltpu.VMEM((KROWS, 256), f32),
            pltpu.VMEM((KROWS, 256), f32),
            pltpu.VMEM((STEP, LANES), f32),
            pltpu.VMEM((STEP, LANES), f32),
        ],
        compiler_params=pltpu.CompilerParams(vmem_limit_bytes=32 * 1024 * 1024),
        cost_estimate=pl.CostEstimate(flops=10**10, bytes_accessed=6 * 10**6, transcendentals=24 * 10**6),
        name="radiate",
    )(sun, coef, rows, factor, cosine, temp, capacity, conduct)


def finish_call(got, base, response):
    return pl.pallas_call(
        finish_kernel,
        out_shape=jax.ShapeDtypeStruct(base.shape, f32),
        name="finish",
    )(got, base, response)


def local(
    absorber, cos_zenith, albedo, absorption, gpoint_weight, sunlit, area_weight,
    land_owner, land_block, land_cell, soil_temp, heat_capacity, conductance,
):
    devices = lax.axis_size(("lon", "lat"))
    path = jnp.transpose(absorber, (1, 0, 2))
    sun = sunlit.T
    rows, factor, coef, send = surface_call(
        sun, land_owner.T, land_block.T, gpoint_weight, absorption, path,
        cos_zenith, albedo, area_weight, land_cell, devices,
    )
    got = lax.all_to_all(send, ("lon", "lat"), 0, 0, tiled=True)
    heat, base, response = radiate_call(
        sun, coef, rows, factor, cos_zenith, soil_temp, heat_capacity, conductance
    )
    return jnp.transpose(heat, (1, 0, 2)), finish_call(got, base, response)


def solution(mesh):
    columns = P("lat", "lon")
    land = P(None, ("lon", "lat"), None)
    in_specs = (
        P("lat", None, "lon"), columns, columns, P(), P(), columns, columns,
        columns, columns, columns, land, land, land,
    )
    out_specs = (P("lat", None, "lon"), land)
    return jax.shard_map(local, mesh=mesh, in_specs=in_specs, out_specs=out_specs, check_vma=False)
```

```python
import functools
import math

import jax
import jax.numpy as jnp
from jax import lax
from jax.experimental import pallas as pl
from jax.experimental.pallas import tpu as pltpu
from jax.sharding import PartitionSpec as P

diffusivity = 1.66
log2e = math.log2(math.e)
f32 = jnp.float32
bf16 = jnp.bfloat16

LANES = 128
GP = 16
LEVELS = 90
KROWS = 96
CHUNKS = 12
STEP = 16


def high_part(x):
    return x.astype(bf16).astype(f32)


def coefficient_rows(absorption, weight_rows):
    scaled = absorption * (diffusivity * log2e)
    high = high_part(scaled)
    low = scaled - high
    offset = jnp.log2(weight_rows) * (-diffusivity)
    first = high_part(offset)
    second = high_part(offset - first)
    third = offset - first - second
    lane = lax.broadcasted_iota(jnp.int32, (GP, 6), 1)
    terms = jnp.where(
        lane == 0, first[:, :6], jnp.where(lane == 1, second[:, :6], jnp.where(lane == 2, third[:, :6], 0.0))
    )
    zeros = jnp.zeros((GP, 6), f32)
    tail = jnp.zeros((GP, 256 - 2 * KROWS), f32)
    return jnp.concatenate([high, terms, low, zeros, tail], axis=1)


def surface_kernel(
    sun, owner, target, weight, absorption, path, cosine, albedo, area, cell,
    rows_out, factor_out, coef_out, send_out,
    wide, weight_rows, coef, mu, nu, alb, contrib,
):
    step = pl.program_id(0)

    @pl.when(step == 0)
    def _():
        for g in range(GP):
            weight_rows[g : g + 1, :] = jnp.full((1, LANES), weight[g], f32)
        rows = coefficient_rows(absorption[...], weight_rows[...])
        coef_out[...] = rows
        coef[...] = rows.astype(bf16)
        send_out[...] = jnp.zeros(send_out.shape, f32)

    cos_f = cosine[...].astype(f32)
    mu[...] = cos_f
    nu[...] = (-1.0 / diffusivity) / cos_f
    alb[...] = albedo[...].astype(f32)
    wide[0 : LEVELS * STEP, :] = path[...].astype(f32).reshape(LEVELS * STEP, LANES)
    for extra in range(LEVELS, KROWS):
        wide[extra * STEP : (extra + 1) * STEP, :] = cos_f
    last = coef[:, : 2 * KROWS]
    for pair in range(STEP // 2):
        cols = []
        for half in range(2):
            block = 2 * pair + half
            rows = wide[pl.ds(block, KROWS, stride=STEP), :].astype(bf16)
            rows_out[block] = rows
            cols.append(rows)
        once = jnp.concatenate(cols, axis=1)
        depth = jnp.dot(last, jnp.concatenate([once, once], axis=0), preferred_element_type=f32)
        for half in range(2):
            block = 2 * pair + half
            part = depth[:, half * LANES : (half + 1) * LANES]
            nu_row = nu[block : block + 1, :]
            alb_row = alb[block : block + 1, :]
            factor_out[block] = alb_row * jnp.exp2(part * (nu_row - 1.0))
            total = jnp.sum(jnp.exp2(part * nu_row), axis=0, keepdims=True)
            flux = (1.0 - alb_row) * mu[block : block + 1, :] * total
            contrib[block : block + 1, :] = area[block : block + 1, :] * flux
    cell_ids = lax.broadcasted_iota(jnp.int32, (LANES, LANES), 0)
    row_ids = lax.broadcasted_iota(jnp.int32, (STEP, 2 * LANES), 0)
    lane_half = lax.broadcasted_iota(jnp.int32, (STEP, 2 * LANES), 1) // LANES
    for pair in range(STEP // 2):
        hots = []
        values = []
        for half in range(2):
            block = 2 * pair + half
            hots.append(jnp.where(cell[block : block + 1, :] == cell_ids, 1.0, 0.0).astype(bf16))
            values.append(jnp.broadcast_to(contrib[block : block + 1, :], (STEP, LANES)))
        value = jnp.concatenate(values, axis=1)
        first = high_part(value)
        second = high_part(value - first)
        third = value - first - second
        which = jnp.where(row_ids // 3 == lane_half, row_ids % 3, 3)
        left = jnp.where(which == 0, first, jnp.where(which == 1, second, jnp.where(which == 2, third, 0.0)))
        sums = lax.dot_general(
            left.astype(bf16),
            jnp.concatenate(hots, axis=1),
            (((1,), (1,)), ((), ())),
            preferred_element_type=f32,
        )
        for half in range(2):
            block = 2 * pair + half
            index = step * STEP + block
            row = sums[3 * half : 3 * half + 1] + sums[3 * half + 1 : 3 * half + 2] + sums[3 * half + 2 : 3 * half + 3]

            @pl.when(sun[0, index] == 1)
            def _():
                to = owner[0, index]
                send_out[to, 0:1, :] = row
                send_out[to, 1:2, :] = jnp.full((1, LANES), target[0, index].astype(f32))


def soil_ahead(temp, capacity, conduct, base_out, response_out):
    layers = temp.shape[0]
    ratio = []
    base = []
    response = []
    for layer in range(layers):
        right = capacity[layer] * temp[layer]
        diagonal = capacity[layer] + conduct[layer]
        if layer == 0:
            inverse = 1.0 / diagonal
            base.append(right * inverse)
            response.append(inverse)
        else:
            above = conduct[layer - 1]
            inverse = 1.0 / (diagonal + above + above * ratio[-1])
            base.append((right + above * base[-1]) * inverse)
            response.append(above * response[-1] * inverse)
        ratio.append(-conduct[layer] * inverse)
    x0 = base[-1]
    x1 = response[-1]
    base_out[layers - 1] = x0
    response_out[layers - 1] = x1
    for layer in range(layers - 2, -1, -1):
        x0 = base[layer] - ratio[layer] * x0
        x1 = response[layer] - ratio[layer] * x1
        base_out[layer] = x0
        response_out[layer] = x1


def radiate_kernel(
    sun, coef, rows, factor, cosine, temp, capacity, conduct,
    heat_out, base_out, response_out,
    weights, depth_a, depth_b, acc_a, acc_b, mu, nu,
):
    step = pl.program_id(0)

    @pl.when(step == 0)
    def _():
        lane = lax.broadcasted_iota(jnp.int32, (8, LANES), 1)
        row = lax.broadcasted_iota(jnp.int32, (8, LANES), 0)
        level_a = jnp.where(lane < LEVELS, lane, jnp.where(lane < KROWS, -1, lane - KROWS))
        level_b = lane + (LANES - KROWS)
        for chunk in range(CHUNKS):
            below_a = level_a < row + 8 * chunk
            below_b = level_b < row + 8 * chunk
            for g in range(0, GP, 2):
                at = (chunk * GP + g) * 8
                for tile, below in ((0, below_a), (1, below_b)):
                    lanes = slice(tile * LANES, (tile + 1) * LANES)
                    both = [jnp.where(below, coef[h : h + 1, lanes], 0.0) for h in (g, g + 1)]
                    weights[at : at + 16, lanes] = jnp.concatenate(both, axis=0).astype(bf16)
        soil_ahead(temp, capacity, conduct, base_out, response_out)

    cos_f = cosine[...].astype(f32)
    mu[...] = cos_f
    nu[...] = (-1.0 / diffusivity) / cos_f
    lit = sun[0, step * STEP]
    for block in range(1, STEP):
        lit = lit | sun[0, step * STEP + block]
    flat = heat_out.reshape(LEVELS * STEP, LANES)

    def depths(pair, depth):
        once = jnp.concatenate([rows[2 * pair], rows[2 * pair + 1]], axis=1)
        twice = jnp.concatenate([once, once], axis=0)
        for part in range(2):
            at = slice(part * 768, (part + 1) * 768)
            depth[at, :] = jnp.dot(weights[at, : 2 * KROWS], twice, preferred_element_type=f32)

    def fluxes(pair, depth, acc):
        for half in range(2):
            block = 2 * pair + half
            lanes = slice(half * LANES, (half + 1) * LANES)
            nu_rows = jnp.broadcast_to(nu[pl.ds(block, 1), :], (8, LANES))
            for chunk in range(CHUNKS):
                total = None
                for g in range(GP):
                    at = (chunk * GP + g) * 8
                    depth_now = depth[at : at + 8, lanes]
                    down = jnp.exp2(depth_now * nu_rows)
                    up = jnp.exp2(depth_now) * factor[block, g : g + 1, :]
                    total = down - up if total is None else (total + down) - up
                acc[chunk * 8 : chunk * 8 + 8, lanes] = total
            keep = (sun[0, step * STEP + block] == 1)
            scale = jnp.where(keep, mu[pl.ds(block, 1), :], 0.0)
            flat[pl.ds(block, LEVELS, stride=STEP), :] = (
                acc[0:LEVELS, lanes] - acc[1 : LEVELS + 1, lanes]
            ) * scale

    @pl.when(lit != 0)
    def _():
        depths(0, depth_a)

        def body(i, _):
            depths(2 * i + 1, depth_b)
            fluxes(2 * i, depth_a, acc_a)
            depths(jnp.minimum(2 * i + 2, STEP // 2 - 1), depth_a)
            fluxes(2 * i + 1, depth_b, acc_b)
            return 0

        lax.fori_loop(0, STEP // 4, body, 0)

    @pl.when(lit == 0)
    def _():
        heat_out[...] = jnp.zeros(heat_out.shape, f32)


def finish_kernel(got, base, response, soil_out):
    senders = got.shape[0] // 2
    values = got[pl.ds(0, senders, stride=2), :]
    ids = got[pl.ds(1, senders, stride=2), :]
    groups = senders // 8
    tiles = [(ids[8 * t : 8 * t + 8], values[8 * t : 8 * t + 8]) for t in range(groups)]
    sums = []
    for block in range(soil_out.shape[1]):
        parts = [jnp.where(i == float(block), v, 0.0) for i, v in tiles]
        while len(parts) > 1:
            parts = [x + y for x, y in zip(parts[::2], parts[1::2])]
        sums.append(jnp.sum(parts[0], axis=0, keepdims=True))
    flux = jnp.concatenate(sums, axis=0)
    soil_out[...] = base[...] + response[...] * flux[None]


def whole(shape):
    return pl.BlockSpec(shape, lambda i: (0,) * len(shape))


def surface_call(sun, owner, target, weight, absorption, path, cosine, albedo, area, cell, devices):
    blocks = path.shape[1]
    smem = pl.BlockSpec(memory_space=pltpu.SMEM)
    by_block = pl.BlockSpec((STEP, LANES), lambda i: (i, 0))
    return pl.pallas_call(
        surface_kernel,
        grid=(blocks // STEP,),
        in_specs=[
            smem, smem, smem, smem,
            whole((GP, LEVELS)),
            pl.BlockSpec((LEVELS, STEP, LANES), lambda i: (0, i, 0)),
            by_block, by_block, by_block, by_block,
        ],
        out_specs=[
            pl.BlockSpec((STEP, KROWS, LANES), lambda i: (i, 0, 0)),
            pl.BlockSpec((STEP, GP, LANES), lambda i: (i, 0, 0)),
            whole((GP, 256)),
            whole((devices, 2, LANES)),
        ],
        out_shape=[
            jax.ShapeDtypeStruct((blocks, KROWS, LANES), bf16),
            jax.ShapeDtypeStruct((blocks, GP, LANES), f32),
            jax.ShapeDtypeStruct((GP, 256), f32),
            jax.ShapeDtypeStruct((devices, 2, LANES), f32),
        ],
        scratch_shapes=[
            pltpu.VMEM((KROWS * STEP, LANES), f32),
            pltpu.VMEM((GP, LANES), f32),
            pltpu.VMEM((GP, 256), bf16),
            pltpu.VMEM((STEP, LANES), f32),
            pltpu.VMEM((STEP, LANES), f32),
            pltpu.VMEM((STEP, LANES), f32),
            pltpu.VMEM((STEP, LANES), f32),
        ],
        compiler_params=pltpu.CompilerParams(vmem_limit_bytes=60 * 1024 * 1024),
        cost_estimate=pl.CostEstimate(flops=10**9, bytes_accessed=4 * 10**6, transcendentals=10**6),
        name="surface",
    )(sun, owner, target, weight, absorption, path, cosine, albedo, area, cell)


def radiate_call(sun, coef, rows, factor, cosine, temp, capacity, conduct):
    blocks = rows.shape[0]
    soil = temp.shape
    return pl.pallas_call(
        radiate_kernel,
        grid=(blocks // STEP,),
        in_specs=[
            pl.BlockSpec(memory_space=pltpu.SMEM),
            whole((GP, 256)),
            pl.BlockSpec((STEP, KROWS, LANES), lambda i: (i, 0, 0)),
            pl.BlockSpec((STEP, GP, LANES), lambda i: (i, 0, 0)),
            pl.BlockSpec((STEP, LANES), lambda i: (i, 0)),
            whole(soil), whole(soil), whole(soil),
        ],
        out_specs=[
            pl.BlockSpec((LEVELS, STEP, LANES), lambda i: (0, i, 0)),
            whole(soil), whole(soil),
        ],
        out_shape=[
            jax.ShapeDtypeStruct((LEVELS, blocks, LANES), f32),
            jax.ShapeDtypeStruct(soil, f32),
            jax.ShapeDtypeStruct(soil, f32),
        ],
        scratch_shapes=[
            pltpu.VMEM((CHUNKS * GP * 8, 256), bf16),
            pltpu.VMEM((CHUNKS * GP * 8, 256), f32),
            pltpu.VMEM((CHUNKS * GP * 8, 256), f32),
            pltpu.VMEM((KROWS, 256), f32),
            pltpu.VMEM((KROWS, 256), f32),
            pltpu.VMEM((STEP, LANES), f32),
            pltpu.VMEM((STEP, LANES), f32),
        ],
        compiler_params=pltpu.CompilerParams(vmem_limit_bytes=60 * 1024 * 1024),
        cost_estimate=pl.CostEstimate(flops=10**10, bytes_accessed=6 * 10**6, transcendentals=24 * 10**6),
        name="radiate",
    )(sun, coef, rows, factor, cosine, temp, capacity, conduct)


def finish_call(got, base, response):
    return pl.pallas_call(
        finish_kernel,
        out_shape=jax.ShapeDtypeStruct(base.shape, f32),
        compiler_params=pltpu.CompilerParams(vmem_limit_bytes=60 * 1024 * 1024),
        name="finish",
    )(got.reshape(-1, LANES), base, response)


def local(
    absorber, cos_zenith, albedo, absorption, gpoint_weight, sunlit, area_weight,
    land_owner, land_block, land_cell, soil_temp, heat_capacity, conductance,
):
    devices = lax.axis_size(("lon", "lat"))
    path = jnp.transpose(absorber, (1, 0, 2))
    sun = sunlit.T
    rows, factor, coef, send = surface_call(
        sun, land_owner.T, land_block.T, gpoint_weight, absorption, path,
        cos_zenith, albedo, area_weight, land_cell, devices,
    )
    got = lax.all_to_all(send, ("lon", "lat"), 0, 0, tiled=True)
    heat, base, response = radiate_call(
        sun, coef, rows, factor, cos_zenith, soil_temp, heat_capacity, conductance
    )
    return jnp.transpose(heat, (1, 0, 2)), finish_call(got, base, response)


def solution(mesh):
    columns = P("lat", "lon")
    land = P(None, ("lon", "lat"), None)
    in_specs = (
        P("lat", None, "lon"), columns, columns, P(), P(), columns, columns,
        columns, columns, columns, land, land, land,
    )
    out_specs = (P("lat", None, "lon"), land)
    return jax.shard_map(local, mesh=mesh, in_specs=in_specs, out_specs=out_specs, check_vma=False)
```

```python
import functools
import math

import jax
import jax.numpy as jnp
from jax import lax
from jax.experimental import pallas as pl
from jax.experimental.pallas import tpu as pltpu
from jax.sharding import PartitionSpec as P

diffusivity = 1.66
log2e = math.log2(math.e)
f32 = jnp.float32
bf16 = jnp.bfloat16

LANES = 128
GP = 16
LEVELS = 90
KROWS = 96
CHUNKS = 12
UNROLL = 8
STEP = 16


def high_part(x):
    return x.astype(bf16).astype(f32)


def coefficient_rows(absorption, weight_rows):
    scaled = absorption * (diffusivity * log2e)
    high = high_part(scaled)
    low = scaled - high
    offset = jnp.log2(weight_rows) * (-diffusivity)
    first = high_part(offset)
    second = high_part(offset - first)
    third = offset - first - second
    lane = lax.broadcasted_iota(jnp.int32, (GP, 6), 1)
    terms = jnp.where(
        lane == 0, first[:, :6], jnp.where(lane == 1, second[:, :6], jnp.where(lane == 2, third[:, :6], 0.0))
    )
    zeros = jnp.zeros((GP, 6), f32)
    tail = jnp.zeros((GP, 256 - 2 * KROWS), f32)
    return jnp.concatenate([high, terms, low, zeros, tail], axis=1)


def surface_kernel(
    sun, owner, target, weight, absorption, path, cosine, albedo, area, cell,
    rows_out, factor_out, coef_out, send_out,
    wide, weight_rows, coef, mu, nu, alb, contrib,
):
    step = pl.program_id(0)

    @pl.when(step == 0)
    def _():
        for g in range(GP):
            weight_rows[g : g + 1, :] = jnp.full((1, LANES), weight[g], f32)
        rows = coefficient_rows(absorption[...], weight_rows[...])
        coef_out[...] = rows
        coef[...] = rows.astype(bf16)
        send_out[...] = jnp.zeros(send_out.shape, f32)

    cos_f = cosine[...].astype(f32)
    mu[...] = cos_f
    nu[...] = (-1.0 / diffusivity) / cos_f
    alb[...] = albedo[...].astype(f32)
    wide[0 : LEVELS * STEP, :] = path[...].astype(f32).reshape(LEVELS * STEP, LANES)
    for extra in range(LEVELS, KROWS):
        wide[extra * STEP : (extra + 1) * STEP, :] = cos_f
    last = coef[:, : 2 * KROWS]
    for pair in range(STEP // 2):
        cols = []
        for half in range(2):
            block = 2 * pair + half
            rows = wide[pl.ds(block, KROWS, stride=STEP), :].astype(bf16)
            rows_out[block] = rows
            cols.append(rows)
        once = jnp.concatenate(cols, axis=1)
        depth = jnp.dot(last, jnp.concatenate([once, once], axis=0), preferred_element_type=f32)
        for half in range(2):
            block = 2 * pair + half
            part = depth[:, half * LANES : (half + 1) * LANES]
            nu_row = nu[block : block + 1, :]
            alb_row = alb[block : block + 1, :]
            factor_out[block] = alb_row * jnp.exp2(part * (nu_row - 1.0))
            total = jnp.sum(jnp.exp2(part * nu_row), axis=0, keepdims=True)
            flux = (1.0 - alb_row) * mu[block : block + 1, :] * total
            contrib[block : block + 1, :] = jnp.where(sun[0, step * STEP + block] == 1, area[block : block + 1, :] * flux, 0.0)
    ready = []
    cell_ids = lax.broadcasted_iota(jnp.int32, (LANES, LANES), 0)
    row_ids = lax.broadcasted_iota(jnp.int32, (STEP, 2 * LANES), 0)
    lane_half = lax.broadcasted_iota(jnp.int32, (STEP, 2 * LANES), 1) // LANES
    for pair in range(STEP // 2):
        hots = []
        values = []
        for half in range(2):
            block = 2 * pair + half
            hots.append(jnp.where(cell[block : block + 1, :] == cell_ids, 1.0, 0.0).astype(bf16))
            values.append(jnp.broadcast_to(contrib[block : block + 1, :], (STEP, LANES)))
        value = jnp.concatenate(values, axis=1)
        first = high_part(value)
        second = high_part(value - first)
        third = value - first - second
        which = jnp.where(row_ids // 3 == lane_half, row_ids % 3, 3)
        left = jnp.where(which == 0, first, jnp.where(which == 1, second, jnp.where(which == 2, third, 0.0)))
        sums = lax.dot_general(
            left.astype(bf16),
            jnp.concatenate(hots, axis=1),
            (((1,), (1,)), ((), ())),
            preferred_element_type=f32,
        )
        for half in range(2):
            block = 2 * pair + half
            index = step * STEP + block
            row = sums[3 * half : 3 * half + 1] + sums[3 * half + 1 : 3 * half + 2] + sums[3 * half + 2 : 3 * half + 3]
            ready.append((owner[0, index], row, jnp.full((1, LANES), target[0, index].astype(f32))))
    for to, row, ident in ready:
        send_out[to, 0:1, :] = row
        send_out[to, 1:2, :] = ident


def radiate_kernel(
    sun, coef, rows, factor, cosine,
    heat_out,
    weights, acc_a, acc_b, mu, nu,
):
    step = pl.program_id(0)

    @pl.when(step == 0)
    def _():
        lane = lax.broadcasted_iota(jnp.int32, (8, LANES), 1)
        row = lax.broadcasted_iota(jnp.int32, (8, LANES), 0)
        level_a = jnp.where(lane < LEVELS, lane, jnp.where(lane < KROWS, -1, lane - KROWS))
        level_b = lane + (LANES - KROWS)
        for chunk in range(CHUNKS):
            below_a = level_a < row + 8 * chunk
            below_b = level_b < row + 8 * chunk
            for g in range(0, GP, 2):
                at = (chunk * GP + g) * 8
                for tile, below in ((0, below_a), (1, below_b)):
                    lanes = slice(tile * LANES, (tile + 1) * LANES)
                    both = [jnp.where(below, coef[h : h + 1, lanes], 0.0) for h in (g, g + 1)]
                    weights[at : at + 16, lanes] = jnp.concatenate(both, axis=0).astype(bf16)

    cos_f = cosine[...].astype(f32)
    mu[...] = cos_f
    nu[...] = (-1.0 / diffusivity) / cos_f
    lit = sun[0, step * STEP]
    for block in range(1, STEP):
        lit = lit | sun[0, step * STEP + block]
    flat = heat_out.reshape(LEVELS * STEP, LANES)

    def fluxes(pair, acc):
        once = jnp.concatenate([rows[2 * pair], rows[2 * pair + 1]], axis=1)
        twice = jnp.concatenate([once, once], axis=0)
        nu_rows = [jnp.broadcast_to(nu[pl.ds(2 * pair + half, 1), :], (8, LANES)) for half in range(2)]
        for chunk in range(CHUNKS):
            at = slice(chunk * GP * 8, (chunk + 1) * GP * 8)
            depth = jnp.dot(weights[at, : 2 * KROWS], twice, preferred_element_type=f32)
            for half in range(2):
                lanes = slice(half * LANES, (half + 1) * LANES)
                total = None
                for g in range(GP):
                    depth_now = depth[g * 8 : g * 8 + 8, lanes]
                    down = jnp.exp2(depth_now * nu_rows[half])
                    up = jnp.exp2(depth_now) * factor[2 * pair + half, g : g + 1, :]
                    total = down - up if total is None else (total + down) - up
                acc[chunk * 8 : chunk * 8 + 8, lanes] = total
        for half in range(2):
            block = 2 * pair + half
            lanes = slice(half * LANES, (half + 1) * LANES)
            keep = sun[0, step * STEP + block] == 1
            scale = jnp.where(keep, mu[pl.ds(block, 1), :], 0.0)
            flat[pl.ds(block, LEVELS, stride=STEP), :] = (
                acc[0:LEVELS, lanes] - acc[1 : LEVELS + 1, lanes]
            ) * scale

    @pl.when(lit != 0)
    def _():
        def body(i, _):
            for u in range(UNROLL):
                fluxes(UNROLL * i + u, (acc_a, acc_b)[u % 2])
            return 0

        lax.fori_loop(0, STEP // 2 // UNROLL, body, 0)

    @pl.when(lit == 0)
    def _():
        heat_out[...] = jnp.zeros(heat_out.shape, f32)


def finish_kernel(got, temp, capacity, conduct, soil_out):
    senders = got.shape[0] // 2
    values = got[pl.ds(0, senders, stride=2), :]
    ids = got[pl.ds(1, senders, stride=2), :]
    tiles = [(ids[8 * t : 8 * t + 8], values[8 * t : 8 * t + 8]) for t in range(senders // 8)]
    sums = []
    for block in range(soil_out.shape[1]):
        parts = [jnp.where(i == float(block), v, 0.0) for i, v in tiles]
        while len(parts) > 1:
            parts = [x + y for x, y in zip(parts[::2], parts[1::2])]
        sums.append(jnp.sum(parts[0], axis=0, keepdims=True))
    flux = jnp.concatenate(sums, axis=0)
    layers = temp.shape[0]
    ratio = []
    inverse = []
    for layer in range(layers):
        pivot = capacity[layer] + conduct[layer]
        if layer > 0:
            above = conduct[layer - 1]
            pivot = (pivot + above) + above * ratio[-1]
        inverse.append(1.0 / pivot)
        ratio.append(-conduct[layer] * inverse[-1])
    scaled = [(capacity[0] * temp[0] + flux) * inverse[0]]
    for layer in range(1, layers):
        right = capacity[layer] * temp[layer] + conduct[layer - 1] * scaled[-1]
        scaled.append(right * inverse[layer])
    solved = scaled[-1]
    soil_out[layers - 1] = solved
    for layer in range(layers - 2, -1, -1):
        solved = scaled[layer] - ratio[layer] * solved
        soil_out[layer] = solved


def whole(shape):
    return pl.BlockSpec(shape, lambda i: (0,) * len(shape))


def surface_call(sun, owner, target, weight, absorption, path, cosine, albedo, area, cell, devices):
    blocks = path.shape[1]
    smem = pl.BlockSpec(memory_space=pltpu.SMEM)
    by_block = pl.BlockSpec((STEP, LANES), lambda i: (i, 0))
    return pl.pallas_call(
        surface_kernel,
        grid=(blocks // STEP,),
        in_specs=[
            smem, smem, smem, smem,
            whole((GP, LEVELS)),
            pl.BlockSpec((LEVELS, STEP, LANES), lambda i: (0, i, 0)),
            by_block, by_block, by_block, by_block,
        ],
        out_specs=[
            pl.BlockSpec((STEP, KROWS, LANES), lambda i: (i, 0, 0)),
            pl.BlockSpec((STEP, GP, LANES), lambda i: (i, 0, 0)),
            whole((GP, 256)),
            whole((devices, 2, LANES)),
        ],
        out_shape=[
            jax.ShapeDtypeStruct((blocks, KROWS, LANES), bf16),
            jax.ShapeDtypeStruct((blocks, GP, LANES), f32),
            jax.ShapeDtypeStruct((GP, 256), f32),
            jax.ShapeDtypeStruct((devices, 2, LANES), f32),
        ],
        scratch_shapes=[
            pltpu.VMEM((KROWS * STEP, LANES), f32),
            pltpu.VMEM((GP, LANES), f32),
            pltpu.VMEM((GP, 256), bf16),
            pltpu.VMEM((STEP, LANES), f32),
            pltpu.VMEM((STEP, LANES), f32),
            pltpu.VMEM((STEP, LANES), f32),
            pltpu.VMEM((STEP, LANES), f32),
        ],
        compiler_params=pltpu.CompilerParams(vmem_limit_bytes=60 * 1024 * 1024),
        cost_estimate=pl.CostEstimate(flops=10**9, bytes_accessed=4 * 10**6, transcendentals=10**6),
        name="surface",
    )(sun, owner, target, weight, absorption, path, cosine, albedo, area, cell)


def radiate_call(sun, coef, rows, factor, cosine):
    blocks = rows.shape[0]
    return pl.pallas_call(
        radiate_kernel,
        grid=(blocks // STEP,),
        in_specs=[
            pl.BlockSpec(memory_space=pltpu.SMEM),
            whole((GP, 256)),
            pl.BlockSpec((STEP, KROWS, LANES), lambda i: (i, 0, 0)),
            pl.BlockSpec((STEP, GP, LANES), lambda i: (i, 0, 0)),
            pl.BlockSpec((STEP, LANES), lambda i: (i, 0)),
        ],
        out_specs=pl.BlockSpec((LEVELS, STEP, LANES), lambda i: (0, i, 0)),
        out_shape=jax.ShapeDtypeStruct((LEVELS, blocks, LANES), f32),
        scratch_shapes=[
            pltpu.VMEM((CHUNKS * GP * 8, 256), bf16),
            pltpu.VMEM((KROWS, 256), f32),
            pltpu.VMEM((KROWS, 256), f32),
            pltpu.VMEM((STEP, LANES), f32),
            pltpu.VMEM((STEP, LANES), f32),
        ],
        compiler_params=pltpu.CompilerParams(vmem_limit_bytes=60 * 1024 * 1024),
        cost_estimate=pl.CostEstimate(flops=10**10, bytes_accessed=6 * 10**6, transcendentals=24 * 10**6),
        name="radiate",
    )(sun, coef, rows, factor, cosine)


def finish_call(got, temp, capacity, conduct):
    return pl.pallas_call(
        finish_kernel,
        out_shape=jax.ShapeDtypeStruct(temp.shape, f32),
        compiler_params=pltpu.CompilerParams(vmem_limit_bytes=4 * 1024 * 1024),
        name="finish",
    )(got.reshape(-1, LANES), temp, capacity, conduct)


def local(
    absorber, cos_zenith, albedo, absorption, gpoint_weight, sunlit, area_weight,
    land_owner, land_block, land_cell, soil_temp, heat_capacity, conductance,
):
    devices = lax.axis_size(("lon", "lat"))
    path = jnp.transpose(absorber, (1, 0, 2))
    sun = sunlit.T
    rows, factor, coef, send = surface_call(
        sun, land_owner.T, land_block.T, gpoint_weight, absorption, path,
        cos_zenith, albedo, area_weight, land_cell, devices,
    )
    got = lax.all_to_all(send, ("lon", "lat"), 0, 0, tiled=True)
    heat = radiate_call(sun, coef, rows, factor, cos_zenith)
    return jnp.transpose(heat, (1, 0, 2)), finish_call(got, soil_temp, heat_capacity, conductance)


def solution(mesh):
    columns = P("lat", "lon")
    land = P(None, ("lon", "lat"), None)
    in_specs = (
        P("lat", None, "lon"), columns, columns, P(), P(), columns, columns,
        columns, columns, columns, land, land, land,
    )
    out_specs = (P("lat", None, "lon"), land)
    return jax.shard_map(local, mesh=mesh, in_specs=in_specs, out_specs=out_specs, check_vma=False)
```

```python
import functools
import math

import jax
import jax.numpy as jnp
from jax import lax
from jax.experimental import pallas as pl
from jax.experimental.pallas import tpu as pltpu
from jax.sharding import PartitionSpec as P

diffusivity = 1.66
log2e = math.log2(math.e)
f32 = jnp.float32
bf16 = jnp.bfloat16

LANES = 128
GP = 16
LEVELS = 90
KROWS = 96
CHUNKS = 11
WIDE = 17
STEP = 16


def high_part(x):
    return x.astype(bf16).astype(f32)


def coefficient_rows(absorption, weight_rows):
    scaled = absorption * (diffusivity * log2e)
    high = high_part(scaled)
    low = scaled - high
    offset = jnp.log2(weight_rows) * (-diffusivity)
    first = high_part(offset)
    second = high_part(offset - first)
    third = offset - first - second
    lane = lax.broadcasted_iota(jnp.int32, (GP, 6), 1)
    terms = jnp.where(
        lane == 0, first[:, :6], jnp.where(lane == 1, second[:, :6], jnp.where(lane == 2, third[:, :6], 0.0))
    )
    zeros = jnp.zeros((GP, 6), f32)
    tail = jnp.zeros((GP, 256 - 2 * KROWS), f32)
    return jnp.concatenate([high, terms, low, zeros, tail], axis=1)


def surface_kernel(
    sun_in, owner_in, target_in, weight_in, absorption_in, path_in, cosine_in, albedo_in, area_in, cell_in,
    rows_to, factor_to, edge_to, coef_to, send_to,
    sun, owner, target, weight, absorption, path, cosine, albedo, area, cell, rows_out, factor_out, edge_out, coef_out, send_out,
    wide, weight_rows, contrib, arrived, left,
):
    blocks = sun.shape[1]
    steps = blocks // STEP
    scalars = [
        pltpu.make_async_copy(a, b, arrived.at[5 + steps + k])
        for k, (a, b) in enumerate(
            [(weight_in, weight), (sun_in, sun), (owner_in, owner), (target_in, target)]
        )
    ]
    small = [
        pltpu.make_async_copy(a, b, arrived.at[k])
        for k, (a, b) in enumerate(
            [
                (absorption_in, absorption), (cosine_in, cosine), (albedo_in, albedo),
                (area_in, area), (cell_in, cell),
            ]
        )
    ]
    paths = [
        pltpu.make_async_copy(path_in.at[:, s * STEP : (s + 1) * STEP, :], path.at[s], arrived.at[5 + s])
        for s in range(steps)
    ]
    for copy in scalars[:1] + small[:3] + scalars[1:2] + paths + small[3:] + scalars[2:]:
        copy.start()
    out = []

    def send(source, place, k):
        copy = pltpu.make_async_copy(source, place, left.at[k])
        copy.start()
        out.append(copy)

    send_out[...] = jnp.zeros(send_out.shape, f32)
    scalars[0].wait()
    top = weight[0]
    for g in range(1, GP):
        top = top + weight[g]
    for g in range(GP):
        weight_rows[g : g + 1, :] = jnp.full((1, LANES), weight[g], f32)
    small[0].wait()
    coef = coefficient_rows(absorption[...], weight_rows[...])
    coef_out[...] = coef
    send(coef_out, coef_to, 0)
    lane = lax.broadcasted_iota(jnp.int32, (GP, 256), 1)
    level = jnp.where(lane < LEVELS, lane, jnp.where(lane < KROWS, -1, lane - KROWS))
    few = jnp.concatenate(
        [coef, jnp.where(level < LEVELS - 1, coef, 0.0), jnp.where(level < 0, coef, 0.0)], axis=0
    ).astype(bf16)[:, : 2 * KROWS]
    small[1].wait()
    small[2].wait()
    scalars[1].wait()
    mu = cosine[...].astype(f32)
    nu = (-1.0 / diffusivity) / mu
    alb = albedo[...].astype(f32)
    for s in range(steps):
        paths[s].wait()
        turn = s % 2
        for extra in range(LEVELS):
            wide[turn, extra * WIDE : extra * WIDE + STEP, :] = path[s, extra].astype(f32)
        for extra in range(LEVELS, KROWS):
            wide[turn, extra * WIDE : extra * WIDE + STEP, :] = mu[s * STEP : (s + 1) * STEP]
        for pair in range(STEP // 2):
            cols = []
            for half in range(2):
                rows = wide[turn, pl.ds(2 * pair + half, KROWS, stride=WIDE), :].astype(bf16)
                rows_out[s * STEP + 2 * pair + half] = rows
                cols.append(rows)
            once = jnp.concatenate(cols, axis=1)
            depth = jnp.dot(few, jnp.concatenate([once, once], axis=0), preferred_element_type=f32)
            for half in range(2):
                block = s * STEP + 2 * pair + half
                part = depth[:, half * LANES : (half + 1) * LANES]
                nu_row = nu[block : block + 1, :]
                alb_row = alb[block : block + 1, :]
                factor = alb_row * jnp.exp2(part[:GP] * (nu_row - 1.0))
                factor_out[block] = factor
                last = (1.0 - alb_row) * jnp.sum(jnp.exp2(part[:GP] * nu_row), axis=0, keepdims=True)
                near = part[GP : 2 * GP]
                near = jnp.exp2(near * nu_row) - factor * jnp.exp2(near)
                first = top - jnp.sum(factor * jnp.exp2(part[2 * GP :]), axis=0, keepdims=True)
                edge_out[block, 0:1, :] = first
                edge_out[block, 1:2, :] = jnp.sum(near, axis=0, keepdims=True)
                edge_out[block, 2:3, :] = last
                contrib[block : block + 1, :] = jnp.where(sun[0, block] == 1, mu[block : block + 1, :] * last, 0.0)
        part = slice(s * STEP, (s + 1) * STEP)
        send(rows_out.at[part], rows_to.at[part], 1 + 3 * s)
        send(factor_out.at[part], factor_to.at[part], 2 + 3 * s)
        send(edge_out.at[part], edge_to.at[part], 3 + 3 * s)
    small[3].wait()
    small[4].wait()
    scalars[2].wait()
    scalars[3].wait()
    ready = []
    cell_ids = lax.broadcasted_iota(jnp.int32, (LANES, LANES), 0)
    row_ids = lax.broadcasted_iota(jnp.int32, (STEP, 2 * LANES), 0)
    lane_half = lax.broadcasted_iota(jnp.int32, (STEP, 2 * LANES), 1) // LANES
    which = jnp.where(row_ids // 3 == lane_half, row_ids % 3, 3)
    for pair in range(blocks // 2):
        hots = []
        values = []
        for half in range(2):
            block = 2 * pair + half
            hots.append(jnp.where(cell[block : block + 1, :] == cell_ids, 1.0, 0.0).astype(bf16))
            value = contrib[block : block + 1, :] * area[block : block + 1, :]
            values.append(jnp.broadcast_to(value, (STEP, LANES)))
        value = jnp.concatenate(values, axis=1)
        first = high_part(value)
        second = high_part(value - first)
        third = value - first - second
        left_rows = jnp.where(which == 0, first, jnp.where(which == 1, second, jnp.where(which == 2, third, 0.0)))
        sums = lax.dot_general(
            left_rows.astype(bf16),
            jnp.concatenate(hots, axis=1),
            (((1,), (1,)), ((), ())),
            preferred_element_type=f32,
        )
        for half in range(2):
            block = 2 * pair + half
            row = sums[3 * half : 3 * half + 1] + sums[3 * half + 1 : 3 * half + 2] + sums[3 * half + 2 : 3 * half + 3]
            ready.append((owner[0, block], row, jnp.full((1, LANES), target[0, block].astype(f32))))
    for to, row, ident in ready:
        send_out[to, 0:1, :] = row
        send_out[to, 1:2, :] = ident
    send(send_out, send_to, 1 + 3 * steps)
    for copy in out:
        copy.wait()


def radiate_kernel(
    sun_in, coef_in, rows_in, factor_in, edge_in, cosine_in,
    heat_to,
    sun, coef, cosine, weights, rows, factor, edge, mu, nu, acc_a, acc_b, heat, arrived, left,
):
    blocks = rows.shape[0]
    steps = blocks // STEP

    def fetch(s):
        part = pl.ds(s * STEP, STEP)
        return [
            pltpu.make_async_copy(a.at[part], b.at[part], arrived.at[k, s])
            for k, (a, b) in enumerate([(rows_in, rows), (factor_in, factor), (edge_in, edge)])
        ]

    def flush(s, slot):
        at = pl.multiple_of(s * STEP, STEP)
        return pltpu.make_async_copy(
            heat.at[slot].reshape(LEVELS, STEP, LANES), heat_to.at[:, pl.ds(at, STEP), :], left.at[slot]
        )

    small = [
        pltpu.make_async_copy(a, b, arrived.at[3, k])
        for k, (a, b) in enumerate([(coef_in, coef), (cosine_in, cosine), (sun_in, sun)])
    ]
    for copy in small:
        copy.start()
    for s in range(steps):
        for copy in fetch(s):
            copy.start()
    for copy in small:
        copy.wait()
    lane = lax.broadcasted_iota(jnp.int32, (8, 256), 1)
    row = lax.broadcasted_iota(jnp.int32, (8, 256), 0)
    level = jnp.where(lane < LEVELS, lane, jnp.where(lane < KROWS, -1, lane - KROWS))
    for chunk in range(CHUNKS):
        below = level < row + 8 * chunk + 1
        for g in range(0, GP, 2):
            at = (chunk * GP + g) * 8
            both = [jnp.where(below, coef[h : h + 1, :], 0.0) for h in (g, g + 1)]
            weights[at : at + 16, :] = jnp.concatenate(both, axis=0).astype(bf16)
    cos_f = cosine[...].astype(f32)
    mu[...] = cos_f
    nu[...] = (-1.0 / diffusivity) / cos_f

    def fluxes(base, pair, acc, slot):
        first = base + 2 * pair
        once = jnp.concatenate([rows[first], rows[first + 1]], axis=1)
        twice = jnp.concatenate([once, once], axis=0)
        nu_rows = [jnp.broadcast_to(nu[pl.ds(first + half, 1), :], (8, LANES)) for half in range(2)]
        for chunk in range(CHUNKS):
            at = slice(chunk * GP * 8, (chunk + 1) * GP * 8)
            depth = jnp.dot(weights[at, : 2 * KROWS], twice, preferred_element_type=f32)
            for half in range(2):
                lanes = slice(half * LANES, (half + 1) * LANES)
                total = None
                for g in range(GP):
                    depth_now = depth[g * 8 : g * 8 + 8, lanes]
                    down = jnp.exp2(depth_now * nu_rows[half])
                    up = jnp.exp2(depth_now) * factor[first + half, g : g + 1, :]
                    total = down - up if total is None else (total + down) - up
                acc[8 + chunk * 8 : 16 + chunk * 8, lanes] = total
        for half in range(2):
            block = first + half
            lanes = slice(half * LANES, (half + 1) * LANES)
            acc[7:8, lanes] = edge[block, 0:1, :]
            acc[96:98, lanes] = edge[block, 1:3, :]
            keep = sun[0, block] == 1
            scale = jnp.where(keep, mu[pl.ds(block, 1), :], 0.0)
            heat[slot, pl.ds(2 * pair + half, LEVELS, stride=STEP), :] = (
                acc[7 : 7 + LEVELS, lanes] - acc[8 : 8 + LEVELS, lanes]
            ) * scale

    def body(s, _):
        slot = s % 2
        base = s * STEP
        for copy in fetch(s):
            copy.wait()

        @pl.when(s >= 2)
        def _():
            flush(s - 2, slot).wait()

        lit = sun[0, base]
        for block in range(1, STEP):
            lit = lit | sun[0, base + block]

        @pl.when(lit != 0)
        def _():
            for pair in range(STEP // 2):
                fluxes(base, pair, (acc_a, acc_b)[pair % 2], slot)

        @pl.when(lit == 0)
        def _():
            heat[slot] = jnp.zeros(heat.shape[1:], f32)

        flush(s, slot).start()
        return 0

    lax.fori_loop(0, steps, body, 0)
    for s in range(max(steps - 2, 0), steps):
        flush(s, s % 2).wait()


def finish_kernel(got, temp, capacity, conduct, soil_out):
    senders = got.shape[0] // 2
    values = got[pl.ds(0, senders, stride=2), :]
    ids = got[pl.ds(1, senders, stride=2), :]
    tiles = [(ids[8 * t : 8 * t + 8], values[8 * t : 8 * t + 8]) for t in range(senders // 8)]
    sums = []
    for block in range(soil_out.shape[1]):
        parts = [jnp.where(i == float(block), v, 0.0) for i, v in tiles]
        while len(parts) > 1:
            parts = [x + y for x, y in zip(parts[::2], parts[1::2])]
        sums.append(jnp.sum(parts[0], axis=0, keepdims=True))
    flux = jnp.concatenate(sums, axis=0)
    layers = temp.shape[0]
    ratio = []
    inverse = []
    for layer in range(layers):
        pivot = capacity[layer] + conduct[layer]
        if layer > 0:
            above = conduct[layer - 1]
            pivot = (pivot + above) + above * ratio[-1]
        inverse.append(1.0 / pivot)
        ratio.append(-conduct[layer] * inverse[-1])
    scaled = [(capacity[0] * temp[0] + flux) * inverse[0]]
    for layer in range(1, layers):
        right = capacity[layer] * temp[layer] + conduct[layer - 1] * scaled[-1]
        scaled.append(right * inverse[layer])
    solved = scaled[-1]
    soil_out[layers - 1] = solved
    for layer in range(layers - 2, -1, -1):
        solved = scaled[layer] - ratio[layer] * solved
        soil_out[layer] = solved


def surface_call(sun, owner, target, weight, absorption, path, cosine, albedo, area, cell, devices):
    blocks = path.shape[1]
    steps = blocks // STEP
    anywhere = pl.BlockSpec(memory_space=pl.ANY)
    shapes = [
        jax.ShapeDtypeStruct((blocks, KROWS, LANES), bf16),
        jax.ShapeDtypeStruct((blocks, GP, LANES), f32),
        jax.ShapeDtypeStruct((blocks, 8, LANES), f32),
        jax.ShapeDtypeStruct((GP, 256), f32),
        jax.ShapeDtypeStruct((devices, 2, LANES), f32),
    ]
    return pl.pallas_call(
        surface_kernel,
        in_specs=[anywhere] * 10,
        out_specs=[anywhere] * 5,
        out_shape=shapes,
        scratch_shapes=[
            pltpu.SMEM((1, blocks), jnp.int32),
            pltpu.SMEM((1, blocks), jnp.int32),
            pltpu.SMEM((1, blocks), jnp.int32),
            pltpu.SMEM((GP,), f32),
            pltpu.VMEM((GP, LEVELS), f32),
            pltpu.VMEM((steps, LEVELS, STEP, LANES), bf16),
            pltpu.VMEM((blocks, LANES), bf16),
            pltpu.VMEM((blocks, LANES), bf16),
            pltpu.VMEM((blocks, LANES), f32),
            pltpu.VMEM((blocks, LANES), jnp.int32),
        ]
        + [pltpu.VMEM(shape.shape, shape.dtype) for shape in shapes]
        + [
            pltpu.VMEM((2, KROWS * WIDE, LANES), f32),
            pltpu.VMEM((GP, LANES), f32),
            pltpu.VMEM((blocks, LANES), f32),
            pltpu.SemaphoreType.DMA((9 + steps,)),
            pltpu.SemaphoreType.DMA((2 + 3 * steps,)),
        ],
        compiler_params=pltpu.CompilerParams(vmem_limit_bytes=60 * 1024 * 1024),
        cost_estimate=pl.CostEstimate(flops=10**9, bytes_accessed=4 * 10**6, transcendentals=10**6),
        name="surface",
    )(sun, owner, target, weight, absorption, path, cosine, albedo, area, cell)


def radiate_call(sun, coef, rows, factor, edge, cosine):
    blocks = rows.shape[0]
    anywhere = pl.BlockSpec(memory_space=pl.ANY)
    return pl.pallas_call(
        radiate_kernel,
        in_specs=[anywhere] * 6,
        out_specs=anywhere,
        out_shape=jax.ShapeDtypeStruct((LEVELS, blocks, LANES), f32),
        scratch_shapes=[
            pltpu.SMEM(sun.shape, jnp.int32),
            pltpu.VMEM(coef.shape, f32),
            pltpu.VMEM(cosine.shape, bf16),
            pltpu.VMEM((CHUNKS * GP * 8, 256), bf16),
            pltpu.VMEM(rows.shape, bf16),
            pltpu.VMEM(factor.shape, f32),
            pltpu.VMEM(edge.shape, f32),
            pltpu.VMEM((blocks, LANES), f32),
            pltpu.VMEM((blocks, LANES), f32),
            pltpu.VMEM((104, 256), f32),
            pltpu.VMEM((104, 256), f32),
            pltpu.VMEM((2, LEVELS * STEP, LANES), f32),
            pltpu.SemaphoreType.DMA((4, max(blocks // STEP, 3))),
            pltpu.SemaphoreType.DMA((2,)),
        ],
        compiler_params=pltpu.CompilerParams(vmem_limit_bytes=60 * 1024 * 1024),
        cost_estimate=pl.CostEstimate(flops=10**10, bytes_accessed=6 * 10**6, transcendentals=24 * 10**6),
        name="radiate",
    )(sun, coef, rows, factor, edge, cosine)


def finish_call(got, temp, capacity, conduct):
    return pl.pallas_call(
        finish_kernel,
        out_shape=jax.ShapeDtypeStruct(temp.shape, f32),
        compiler_params=pltpu.CompilerParams(vmem_limit_bytes=4 * 1024 * 1024),
        name="finish",
    )(got.reshape(-1, LANES), temp, capacity, conduct)


def local(
    absorber, cos_zenith, albedo, absorption, gpoint_weight, sunlit, area_weight,
    land_owner, land_block, land_cell, soil_temp, heat_capacity, conductance,
):
    devices = lax.axis_size(("lon", "lat"))
    path = jnp.transpose(absorber, (1, 0, 2))
    sun = sunlit.T
    rows, factor, edge, coef, send = surface_call(
        sun, land_owner.T, land_block.T, gpoint_weight, absorption, path,
        cos_zenith, albedo, area_weight, land_cell, devices,
    )
    got = lax.all_to_all(send, ("lon", "lat"), 0, 0, tiled=True)
    heat = radiate_call(sun, coef, rows, factor, edge, cos_zenith)
    return jnp.transpose(heat, (1, 0, 2)), finish_call(got, soil_temp, heat_capacity, conductance)


def solution(mesh):
    columns = P("lat", "lon")
    land = P(None, ("lon", "lat"), None)
    in_specs = (
        P("lat", None, "lon"), columns, columns, P(), P(), columns, columns,
        columns, columns, columns, land, land, land,
    )
    out_specs = (P("lat", None, "lon"), land)
    return jax.shard_map(local, mesh=mesh, in_specs=in_specs, out_specs=out_specs, check_vma=False)
```

```python
import functools
import math

import jax
import jax.numpy as jnp
from jax import lax
from jax.experimental import pallas as pl
from jax.experimental.pallas import tpu as pltpu
from jax.sharding import PartitionSpec as P

diffusivity = 1.66
log2e = math.log2(math.e)
f32 = jnp.float32
bf16 = jnp.bfloat16

LANES = 128
GP = 16
LEVELS = 90
KROWS = 96
CHUNKS = 11
WIDE = 17
STEP = 16


def high_part(x):
    return x.astype(bf16).astype(f32)


def coefficient_rows(absorption, weight_rows):
    scaled = absorption * (diffusivity * log2e)
    high = high_part(scaled)
    low = scaled - high
    offset = jnp.log2(weight_rows) * (-diffusivity)
    first = high_part(offset)
    second = high_part(offset - first)
    third = offset - first - second
    lane = lax.broadcasted_iota(jnp.int32, (GP, 6), 1)
    terms = jnp.where(
        lane == 0, first[:, :6], jnp.where(lane == 1, second[:, :6], jnp.where(lane == 2, third[:, :6], 0.0))
    )
    zeros = jnp.zeros((GP, 6), f32)
    tail = jnp.zeros((GP, 256 - 2 * KROWS), f32)
    return jnp.concatenate([high, terms, low, zeros, tail], axis=1)


def surface_kernel(
    sun_in, owner_in, target_in, weight_in, absorption_in, path_in, cosine_in, albedo_in, area_in, cell_in,
    rows_to, factor_to, edge_to, coef_to, send_to,
    sun, owner, target, weight, absorption, path, cosine, albedo, area, cell, rows_out, factor_out, edge_out, coef_out, send_out,
    wide, weight_rows, contrib, arrived, left,
):
    blocks = sun.shape[1]
    steps = blocks // STEP
    scalars = [
        pltpu.make_async_copy(a, b, arrived.at[5 + steps + k])
        for k, (a, b) in enumerate(
            [(weight_in, weight), (sun_in, sun), (owner_in, owner), (target_in, target)]
        )
    ]
    small = [
        pltpu.make_async_copy(a, b, arrived.at[k])
        for k, (a, b) in enumerate(
            [
                (absorption_in, absorption), (cosine_in, cosine), (albedo_in, albedo),
                (area_in, area), (cell_in, cell),
            ]
        )
    ]
    paths = [
        pltpu.make_async_copy(path_in.at[:, s * STEP : (s + 1) * STEP, :], path.at[s], arrived.at[5 + s])
        for s in range(steps)
    ]
    for copy in scalars[:1] + small[:3] + scalars[1:2] + paths + small[3:] + scalars[2:]:
        copy.start()
    out = []

    def send(source, place, k):
        copy = pltpu.make_async_copy(source, place, left.at[k])
        copy.start()
        out.append(copy)

    send_out[...] = jnp.zeros(send_out.shape, f32)
    scalars[0].wait()
    top = weight[0]
    for g in range(1, GP):
        top = top + weight[g]
    for g in range(GP):
        weight_rows[g : g + 1, :] = jnp.full((1, LANES), weight[g], f32)
    small[0].wait()
    coef = coefficient_rows(absorption[...], weight_rows[...])
    coef_out[...] = coef
    send(coef_out, coef_to, 0)
    lane = lax.broadcasted_iota(jnp.int32, (GP, 256), 1)
    level = jnp.where(lane < LEVELS, lane, jnp.where(lane < KROWS, -1, lane - KROWS))
    few = jnp.concatenate(
        [coef, jnp.where(level < LEVELS - 1, coef, 0.0), jnp.where(level < 0, coef, 0.0)], axis=0
    ).astype(bf16)[:, : 2 * KROWS]
    small[1].wait()
    small[2].wait()
    scalars[1].wait()
    mu = cosine[...].astype(f32)
    nu = (-1.0 / diffusivity) / mu
    alb = albedo[...].astype(f32)
    for s in range(steps):
        paths[s].wait()
        turn = s % 2
        for extra in range(LEVELS):
            wide[turn, extra * WIDE : extra * WIDE + STEP, :] = path[s, extra].astype(f32)
        for extra in range(LEVELS, KROWS):
            wide[turn, extra * WIDE : extra * WIDE + STEP, :] = mu[s * STEP : (s + 1) * STEP]
        for pair in range(STEP // 2):
            cols = []
            for half in range(2):
                rows = wide[turn, pl.ds(2 * pair + half, KROWS, stride=WIDE), :].astype(bf16)
                rows_out[s * STEP + 2 * pair + half] = rows
                cols.append(rows)
            once = jnp.concatenate(cols, axis=1)
            depth = jnp.dot(few, jnp.concatenate([once, once], axis=0), preferred_element_type=f32)
            for half in range(2):
                block = s * STEP + 2 * pair + half
                part = depth[:, half * LANES : (half + 1) * LANES]
                nu_row = nu[block : block + 1, :]
                alb_row = alb[block : block + 1, :]
                factor = alb_row * jnp.exp2(part[:GP] * (nu_row - 1.0))
                factor_out[block] = factor
                last = (1.0 - alb_row) * jnp.sum(jnp.exp2(part[:GP] * nu_row), axis=0, keepdims=True)
                near = part[GP : 2 * GP]
                near = jnp.exp2(near * nu_row) - factor * jnp.exp2(near)
                first = top - jnp.sum(factor * jnp.exp2(part[2 * GP :]), axis=0, keepdims=True)
                edge_out[block, 0:1, :] = first
                edge_out[block, 1:2, :] = jnp.sum(near, axis=0, keepdims=True)
                edge_out[block, 2:3, :] = last
                contrib[block : block + 1, :] = jnp.where(sun[0, block] == 1, mu[block : block + 1, :] * last, 0.0)
        part = slice(s * STEP, (s + 1) * STEP)
        send(rows_out.at[part], rows_to.at[part], 1 + 3 * s)
        send(factor_out.at[part], factor_to.at[part], 2 + 3 * s)
        send(edge_out.at[part], edge_to.at[part], 3 + 3 * s)
    small[3].wait()
    small[4].wait()
    scalars[2].wait()
    scalars[3].wait()
    ready = []
    cell_ids = lax.broadcasted_iota(jnp.int32, (LANES, LANES), 0)
    row_ids = lax.broadcasted_iota(jnp.int32, (STEP, 2 * LANES), 0)
    lane_half = lax.broadcasted_iota(jnp.int32, (STEP, 2 * LANES), 1) // LANES
    which = jnp.where(row_ids // 3 == lane_half, row_ids % 3, 3)
    for pair in range(blocks // 2):
        hots = []
        values = []
        for half in range(2):
            block = 2 * pair + half
            hots.append(jnp.where(cell[block : block + 1, :] == cell_ids, 1.0, 0.0).astype(bf16))
            value = contrib[block : block + 1, :] * area[block : block + 1, :]
            values.append(jnp.broadcast_to(value, (STEP, LANES)))
        value = jnp.concatenate(values, axis=1)
        first = high_part(value)
        second = high_part(value - first)
        third = value - first - second
        left_rows = jnp.where(which == 0, first, jnp.where(which == 1, second, jnp.where(which == 2, third, 0.0)))
        sums = lax.dot_general(
            left_rows.astype(bf16),
            jnp.concatenate(hots, axis=1),
            (((1,), (1,)), ((), ())),
            preferred_element_type=f32,
        )
        for half in range(2):
            block = 2 * pair + half
            row = sums[3 * half : 3 * half + 1] + sums[3 * half + 1 : 3 * half + 2] + sums[3 * half + 2 : 3 * half + 3]
            ready.append((owner[0, block], row, jnp.full((1, LANES), target[0, block].astype(f32))))
    for to, row, ident in ready:
        send_out[to, 0:1, :] = row
        send_out[to, 1:2, :] = ident
    send(send_out, send_to, 1 + 3 * steps)
    for copy in out:
        copy.wait()


def radiate_kernel(
    sun_in, coef_in, rows_in, factor_in, edge_in, cosine_in,
    heat_to,
    sun, coef, cosine, weights, rows, factor, edge, mu, nu, acc_a, acc_b, heat, arrived, left,
):
    blocks = rows.shape[0]
    steps = blocks // STEP

    def fetch(s):
        part = pl.ds(s * STEP, STEP)
        return [
            pltpu.make_async_copy(a.at[part], b.at[part], arrived.at[k, s])
            for k, (a, b) in enumerate([(rows_in, rows), (factor_in, factor), (edge_in, edge)])
        ]

    def flush(s, slot):
        at = pl.multiple_of(s * STEP, STEP)
        return pltpu.make_async_copy(
            heat.at[slot, pl.ds(0, LEVELS * STEP)].reshape(LEVELS, STEP, LANES), heat_to.at[:, pl.ds(at, STEP), :], left.at[slot]
        )

    small = [
        pltpu.make_async_copy(a, b, arrived.at[3, k])
        for k, (a, b) in enumerate([(coef_in, coef), (cosine_in, cosine), (sun_in, sun)])
    ]
    for copy in small:
        copy.start()
    for s in range(steps):
        for copy in fetch(s):
            copy.start()
    for copy in small:
        copy.wait()
    lane = lax.broadcasted_iota(jnp.int32, (8, 256), 1)
    row = lax.broadcasted_iota(jnp.int32, (8, 256), 0)
    level = jnp.where(lane < LEVELS, lane, jnp.where(lane < KROWS, -1, lane - KROWS))
    for chunk in range(CHUNKS):
        below = level < row + 8 * chunk + 1
        for g in range(0, GP, 2):
            at = (chunk * GP + g) * 8
            both = [jnp.where(below, coef[h : h + 1, :], 0.0) for h in (g, g + 1)]
            weights[at : at + 16, :] = jnp.concatenate(both, axis=0).astype(bf16)
    cos_f = cosine[...].astype(f32)
    mu[...] = cos_f
    nu[...] = (-1.0 / diffusivity) / cos_f

    def fluxes(base, pair, acc, slot):
        first = base + 2 * pair
        once = jnp.concatenate([rows[first], rows[first + 1]], axis=1)
        twice = jnp.concatenate([once, once], axis=0)
        nu_rows = [jnp.broadcast_to(nu[pl.ds(first + half, 1), :], (8, LANES)) for half in range(2)]
        for chunk in range(CHUNKS):
            at = slice(chunk * GP * 8, (chunk + 1) * GP * 8)
            depth = jnp.dot(weights[at, : 2 * KROWS], twice, preferred_element_type=f32)
            for half in range(2):
                lanes = slice(half * LANES, (half + 1) * LANES)
                total = None
                for g in range(GP):
                    depth_now = depth[g * 8 : g * 8 + 8, lanes]
                    down = jnp.exp2(depth_now * nu_rows[half])
                    up = jnp.exp2(depth_now) * factor[first + half, g : g + 1, :]
                    total = down - up if total is None else (total + down) - up
                acc[8 + chunk * 8 : 16 + chunk * 8, lanes] = total
        for half in range(2):
            block = first + half
            lanes = slice(half * LANES, (half + 1) * LANES)
            acc[7:8, lanes] = edge[block, 0:1, :]
            acc[96:98, lanes] = edge[block, 1:3, :]
            keep = sun[0, block] == 1
            scale = jnp.where(keep, mu[pl.ds(block, 1), :], 0.0)
            heat[slot, pl.ds(2 * pair + half, LEVELS, stride=STEP), :] = (
                acc[7 : 7 + LEVELS, lanes] - acc[8 : 8 + LEVELS, lanes]
            ) * scale

    def body(s, _):
        base = s * (STEP * 2)
        for sub in range(2):
            for copy in fetch(s * 2 + sub):
                copy.wait()
        lit = sun[0, base]
        for block in range(1, STEP * 2):
            lit = lit | sun[0, base + block]

        @pl.when(lit != 0)
        def _():
            for sub in range(2):
                for pair in range(STEP // 2):
                    fluxes(base + sub * STEP, pair, (acc_a, acc_b)[pair % 2], s * 2 + sub)
                flush(s * 2 + sub, s * 2 + sub).start()

        @pl.when(lit == 0)
        def _():
            for sub in range(2):
                heat[s * 2 + sub] = jnp.zeros(heat.shape[1:], f32)
                flush(s * 2 + sub, s * 2 + sub).start()

        return 0

    lax.fori_loop(0, steps // 2, body, 0)
    for s in range(steps):
        flush(s, s).wait()


def finish_kernel(got, temp, capacity, conduct, soil_out):
    senders = got.shape[0] // 2
    values = got[pl.ds(0, senders, stride=2), :]
    ids = got[pl.ds(1, senders, stride=2), :]
    tiles = [(ids[8 * t : 8 * t + 8], values[8 * t : 8 * t + 8]) for t in range(senders // 8)]
    sums = []
    for block in range(soil_out.shape[1]):
        parts = [jnp.where(i == float(block), v, 0.0) for i, v in tiles]
        while len(parts) > 1:
            parts = [x + y for x, y in zip(parts[::2], parts[1::2])]
        sums.append(jnp.sum(parts[0], axis=0, keepdims=True))
    flux = jnp.concatenate(sums, axis=0)
    layers = temp.shape[0]
    ratio = []
    inverse = []
    for layer in range(layers):
        pivot = capacity[layer] + conduct[layer]
        if layer > 0:
            above = conduct[layer - 1]
            pivot = (pivot + above) + above * ratio[-1]
        inverse.append(1.0 / pivot)
        ratio.append(-conduct[layer] * inverse[-1])
    scaled = [(capacity[0] * temp[0] + flux) * inverse[0]]
    for layer in range(1, layers):
        right = capacity[layer] * temp[layer] + conduct[layer - 1] * scaled[-1]
        scaled.append(right * inverse[layer])
    solved = scaled[-1]
    soil_out[layers - 1] = solved
    for layer in range(layers - 2, -1, -1):
        solved = scaled[layer] - ratio[layer] * solved
        soil_out[layer] = solved


def surface_call(sun, owner, target, weight, absorption, path, cosine, albedo, area, cell, devices):
    blocks = path.shape[1]
    steps = blocks // STEP
    anywhere = pl.BlockSpec(memory_space=pl.ANY)
    shapes = [
        jax.ShapeDtypeStruct((blocks, KROWS, LANES), bf16),
        jax.ShapeDtypeStruct((blocks, GP, LANES), f32),
        jax.ShapeDtypeStruct((blocks, 8, LANES), f32),
        jax.ShapeDtypeStruct((GP, 256), f32),
        jax.ShapeDtypeStruct((devices, 2, LANES), f32),
    ]
    return pl.pallas_call(
        surface_kernel,
        in_specs=[anywhere] * 10,
        out_specs=[anywhere] * 5,
        out_shape=shapes,
        scratch_shapes=[
            pltpu.SMEM((1, blocks), jnp.int32),
            pltpu.SMEM((1, blocks), jnp.int32),
            pltpu.SMEM((1, blocks), jnp.int32),
            pltpu.SMEM((GP,), f32),
            pltpu.VMEM((GP, LEVELS), f32),
            pltpu.VMEM((steps, LEVELS, STEP, LANES), bf16),
            pltpu.VMEM((blocks, LANES), bf16),
            pltpu.VMEM((blocks, LANES), bf16),
            pltpu.VMEM((blocks, LANES), f32),
            pltpu.VMEM((blocks, LANES), jnp.int32),
        ]
        + [pltpu.VMEM(shape.shape, shape.dtype) for shape in shapes]
        + [
            pltpu.VMEM((2, KROWS * WIDE + 32, LANES), f32),
            pltpu.VMEM((GP, LANES), f32),
            pltpu.VMEM((blocks, LANES), f32),
            pltpu.SemaphoreType.DMA((9 + steps,)),
            pltpu.SemaphoreType.DMA((2 + 3 * steps,)),
        ],
        compiler_params=pltpu.CompilerParams(vmem_limit_bytes=60 * 1024 * 1024),
        cost_estimate=pl.CostEstimate(flops=10**9, bytes_accessed=4 * 10**6, transcendentals=10**6),
        name="surface",
    )(sun, owner, target, weight, absorption, path, cosine, albedo, area, cell)


def radiate_call(sun, coef, rows, factor, edge, cosine):
    blocks = rows.shape[0]
    anywhere = pl.BlockSpec(memory_space=pl.ANY)
    return pl.pallas_call(
        radiate_kernel,
        in_specs=[anywhere] * 6,
        out_specs=anywhere,
        out_shape=jax.ShapeDtypeStruct((LEVELS, blocks, LANES), f32),
        scratch_shapes=[
            pltpu.SMEM(sun.shape, jnp.int32),
            pltpu.VMEM(coef.shape, f32),
            pltpu.VMEM(cosine.shape, bf16),
            pltpu.VMEM((CHUNKS * GP * 8, 256), bf16),
            pltpu.VMEM(rows.shape, bf16),
            pltpu.VMEM(factor.shape, f32),
            pltpu.VMEM(edge.shape, f32),
            pltpu.VMEM((blocks, LANES), f32),
            pltpu.VMEM((blocks, LANES), f32),
            pltpu.VMEM((104, 256), f32),
            pltpu.VMEM((104, 256), f32),
            pltpu.VMEM((blocks // STEP, KROWS * STEP, LANES), f32),
            pltpu.SemaphoreType.DMA((4, max(blocks // STEP, 3))),
            pltpu.SemaphoreType.DMA((blocks // STEP,)),
        ],
        compiler_params=pltpu.CompilerParams(vmem_limit_bytes=60 * 1024 * 1024),
        cost_estimate=pl.CostEstimate(flops=10**10, bytes_accessed=6 * 10**6, transcendentals=24 * 10**6),
        name="radiate",
    )(sun, coef, rows, factor, edge, cosine)


def finish_call(got, temp, capacity, conduct):
    return pl.pallas_call(
        finish_kernel,
        out_shape=jax.ShapeDtypeStruct(temp.shape, f32),
        compiler_params=pltpu.CompilerParams(vmem_limit_bytes=4 * 1024 * 1024),
        name="finish",
    )(got.reshape(-1, LANES), temp, capacity, conduct)


def local(
    absorber, cos_zenith, albedo, absorption, gpoint_weight, sunlit, area_weight,
    land_owner, land_block, land_cell, soil_temp, heat_capacity, conductance,
):
    devices = lax.axis_size(("lon", "lat"))
    path = jnp.transpose(absorber, (1, 0, 2))
    sun = sunlit.T
    rows, factor, edge, coef, send = surface_call(
        sun, land_owner.T, land_block.T, gpoint_weight, absorption, path,
        cos_zenith, albedo, area_weight, land_cell, devices,
    )
    got = lax.all_to_all(send, ("lon", "lat"), 0, 0, tiled=True)
    heat = radiate_call(sun, coef, rows, factor, edge, cos_zenith)
    return jnp.transpose(heat, (1, 0, 2)), finish_call(got, soil_temp, heat_capacity, conductance)


def solution(mesh):
    columns = P("lat", "lon")
    land = P(None, ("lon", "lat"), None)
    in_specs = (
        P("lat", None, "lon"), columns, columns, P(), P(), columns, columns,
        columns, columns, columns, land, land, land,
    )
    out_specs = (P("lat", None, "lon"), land)
    return jax.shard_map(local, mesh=mesh, in_specs=in_specs, out_specs=out_specs, check_vma=False)
```

```python
import functools
import math

import jax
import jax.numpy as jnp
from jax import lax
from jax.experimental import pallas as pl
from jax.experimental.pallas import tpu as pltpu
from jax.sharding import PartitionSpec as P

diffusivity = 1.66
log2e = math.log2(math.e)
f32 = jnp.float32
bf16 = jnp.bfloat16

LANES = 128
GP = 16
LEVELS = 90
KROWS = 96
CHUNKS = 11
WIDE = 17
STEP = 16


def high_part(x):
    return x.astype(bf16).astype(f32)


def coefficient_rows(absorption, weight_rows):
    scaled = absorption * (diffusivity * log2e)
    high = high_part(scaled)
    low = scaled - high
    offset = jnp.log2(weight_rows) * (-diffusivity)
    first = high_part(offset)
    second = high_part(offset - first)
    third = offset - first - second
    lane = lax.broadcasted_iota(jnp.int32, (GP, 6), 1)
    terms = jnp.where(
        lane == 0, first[:, :6], jnp.where(lane == 1, second[:, :6], jnp.where(lane == 2, third[:, :6], 0.0))
    )
    zeros = jnp.zeros((GP, 6), f32)
    tail = jnp.zeros((GP, 256 - 2 * KROWS), f32)
    return jnp.concatenate([high, terms, low, zeros, tail], axis=1)


def surface_kernel(
    sun_in, owner_in, target_in, weight_in, absorption_in, path_in, cosine_in, albedo_in, area_in, cell_in,
    rows_to, factor_to, edge_to, coef_to, send_to,
    sun, owner, target, weight, absorption, path, cosine, albedo, area, cell, rows_out, factor_out, edge_out, coef_out, send_out,
    wide, weight_rows, contrib, arrived, left,
):
    blocks = sun.shape[1]
    steps = blocks // STEP
    scalars = [
        pltpu.make_async_copy(a, b, arrived.at[5 + steps + k])
        for k, (a, b) in enumerate(
            [(weight_in, weight), (sun_in, sun), (owner_in, owner), (target_in, target)]
        )
    ]
    small = [
        pltpu.make_async_copy(a, b, arrived.at[k])
        for k, (a, b) in enumerate(
            [
                (absorption_in, absorption), (cosine_in, cosine), (albedo_in, albedo),
                (area_in, area), (cell_in, cell),
            ]
        )
    ]
    paths = [
        pltpu.make_async_copy(path_in.at[:, s * STEP : (s + 1) * STEP, :], path.at[s], arrived.at[5 + s])
        for s in range(steps)
    ]
    for copy in scalars[:1] + small[:3] + scalars[1:2] + paths + small[3:] + scalars[2:]:
        copy.start()
    out = []

    def send(source, place, k):
        copy = pltpu.make_async_copy(source, place, left.at[k])
        copy.start()
        out.append(copy)

    send_out[...] = jnp.zeros(send_out.shape, f32)
    scalars[0].wait()
    top = weight[0]
    for g in range(1, GP):
        top = top + weight[g]
    for g in range(GP):
        weight_rows[g : g + 1, :] = jnp.full((1, LANES), weight[g], f32)
    small[0].wait()
    coef = coefficient_rows(absorption[...], weight_rows[...])
    coef_out[...] = coef
    send(coef_out, coef_to, 0)
    lane = lax.broadcasted_iota(jnp.int32, (GP, 256), 1)
    level = jnp.where(lane < LEVELS, lane, jnp.where(lane < KROWS, -1, lane - KROWS))
    few = jnp.concatenate(
        [coef, jnp.where(level < LEVELS - 1, coef, 0.0), jnp.where(level < 0, coef, 0.0)], axis=0
    ).astype(bf16)[:, : 2 * KROWS]
    small[1].wait()
    small[2].wait()
    scalars[1].wait()
    mu = cosine[...].astype(f32)
    nu = (-1.0 / diffusivity) / mu
    alb = albedo[...].astype(f32)
    for s in range(steps):
        paths[s].wait()
        turn = s % 2
        for extra in range(LEVELS):
            wide[turn, extra * WIDE : extra * WIDE + STEP, :] = path[s, extra].astype(f32)
        for extra in range(LEVELS, KROWS):
            wide[turn, extra * WIDE : extra * WIDE + STEP, :] = mu[s * STEP : (s + 1) * STEP]
        for pair in range(STEP // 2):
            cols = []
            for half in range(2):
                rows = wide[turn, pl.ds(2 * pair + half, KROWS, stride=WIDE), :].astype(bf16)
                rows_out[s * STEP + 2 * pair + half] = rows
                cols.append(rows)
            once = jnp.concatenate(cols, axis=1)
            depth = jnp.dot(few, jnp.concatenate([once, once], axis=0), preferred_element_type=f32)
            for half in range(2):
                block = s * STEP + 2 * pair + half
                part = depth[:, half * LANES : (half + 1) * LANES]
                nu_row = nu[block : block + 1, :]
                alb_row = alb[block : block + 1, :]
                factor = alb_row * jnp.exp2(part[:GP] * (nu_row - 1.0))
                factor_out[block] = factor
                last = (1.0 - alb_row) * jnp.sum(jnp.exp2(part[:GP] * nu_row), axis=0, keepdims=True)
                near = part[GP : 2 * GP]
                near = jnp.exp2(near * nu_row) - factor * jnp.exp2(near)
                first = top - jnp.sum(factor * jnp.exp2(part[2 * GP :]), axis=0, keepdims=True)
                edge_out[block, 0:1, :] = first
                edge_out[block, 1:2, :] = jnp.sum(near, axis=0, keepdims=True)
                edge_out[block, 2:3, :] = last
                contrib[block : block + 1, :] = jnp.where(sun[0, block] == 1, mu[block : block + 1, :] * last, 0.0)
        part = slice(s * STEP, (s + 1) * STEP)
        send(rows_out.at[part], rows_to.at[part], 1 + 3 * s)
        send(factor_out.at[part], factor_to.at[part], 2 + 3 * s)
        send(edge_out.at[part], edge_to.at[part], 3 + 3 * s)
    small[3].wait()
    small[4].wait()
    scalars[2].wait()
    scalars[3].wait()
    ready = []
    cell_ids = lax.broadcasted_iota(jnp.int32, (LANES, LANES), 0)
    row_ids = lax.broadcasted_iota(jnp.int32, (STEP, 2 * LANES), 0)
    lane_half = lax.broadcasted_iota(jnp.int32, (STEP, 2 * LANES), 1) // LANES
    which = jnp.where(row_ids // 3 == lane_half, row_ids % 3, 3)
    for pair in range(blocks // 2):
        hots = []
        values = []
        for half in range(2):
            block = 2 * pair + half
            hots.append(jnp.where(cell[block : block + 1, :] == cell_ids, 1.0, 0.0).astype(bf16))
            value = contrib[block : block + 1, :] * area[block : block + 1, :]
            values.append(jnp.broadcast_to(value, (STEP, LANES)))
        value = jnp.concatenate(values, axis=1)
        first = high_part(value)
        second = high_part(value - first)
        third = value - first - second
        left_rows = jnp.where(which == 0, first, jnp.where(which == 1, second, jnp.where(which == 2, third, 0.0)))
        sums = lax.dot_general(
            left_rows.astype(bf16),
            jnp.concatenate(hots, axis=1),
            (((1,), (1,)), ((), ())),
            preferred_element_type=f32,
        )
        for half in range(2):
            block = 2 * pair + half
            row = sums[3 * half : 3 * half + 1] + sums[3 * half + 1 : 3 * half + 2] + sums[3 * half + 2 : 3 * half + 3]
            ready.append((owner[0, block], row, jnp.full((1, LANES), target[0, block].astype(f32))))
    for to, row, ident in ready:
        send_out[to, 0:1, :] = row
        send_out[to, 1:2, :] = ident
    send(send_out, send_to, 1 + 3 * steps)
    for copy in out:
        copy.wait()


def radiate_kernel(
    sun_in, coef_in, rows_in, factor_in, edge_in, cosine_in,
    heat_to,
    sun, coef, cosine, weights, rows, factor, edge, mu, nu, acc_a, acc_b, heat, arrived, left,
):
    blocks = rows.shape[0]
    steps = blocks // STEP

    def fetch(s):
        part = pl.ds(s * STEP, STEP)
        return [
            pltpu.make_async_copy(a.at[part], b.at[part], arrived.at[k, s])
            for k, (a, b) in enumerate([(rows_in, rows), (factor_in, factor), (edge_in, edge)])
        ]

    def flush(s, part):
        at = pl.multiple_of(s * STEP + part * 8, 8)
        result = heat.at[s, pl.ds(0, LEVELS * STEP)].reshape(LEVELS, STEP, LANES)
        return pltpu.make_async_copy(
            result.at[:, pl.ds(part * 8, 8), :], heat_to.at[:, pl.ds(at, 8), :], left.at[s, part]
        )

    small = [
        pltpu.make_async_copy(a, b, arrived.at[3, k])
        for k, (a, b) in enumerate([(coef_in, coef), (cosine_in, cosine), (sun_in, sun)])
    ]
    for copy in small:
        copy.start()
    for s in range(steps):
        for copy in fetch(s):
            copy.start()
    for copy in small:
        copy.wait()
    lane = lax.broadcasted_iota(jnp.int32, (8, 256), 1)
    row = lax.broadcasted_iota(jnp.int32, (8, 256), 0)
    level = jnp.where(lane < LEVELS, lane, jnp.where(lane < KROWS, -1, lane - KROWS))
    for chunk in range(CHUNKS):
        below = level < row + 8 * chunk + 1
        for g in range(0, GP, 2):
            at = (chunk * GP + g) * 8
            both = [jnp.where(below, coef[h : h + 1, :], 0.0) for h in (g, g + 1)]
            weights[at : at + 16, :] = jnp.concatenate(both, axis=0).astype(bf16)
    cos_f = cosine[...].astype(f32)
    mu[...] = cos_f
    nu[...] = (-1.0 / diffusivity) / cos_f

    def fluxes(base, pair, acc, slot):
        first = base + 2 * pair
        once = jnp.concatenate([rows[first], rows[first + 1]], axis=1)
        twice = jnp.concatenate([once, once], axis=0)
        nu_rows = [jnp.broadcast_to(nu[pl.ds(first + half, 1), :], (8, LANES)) for half in range(2)]
        for chunk in range(CHUNKS):
            if chunk % 4 == 0:
                at = slice(chunk * GP * 8, min(chunk + 4, CHUNKS) * GP * 8)
                several = jnp.dot(weights[at, : 2 * KROWS], twice, preferred_element_type=f32)
            depth = several[(chunk % 4) * GP * 8 : (chunk % 4 + 1) * GP * 8]
            for half in range(2):
                lanes = slice(half * LANES, (half + 1) * LANES)
                total = None
                for g in range(GP):
                    depth_now = depth[g * 8 : g * 8 + 8, lanes]
                    down = jnp.exp2(depth_now * nu_rows[half])
                    up = jnp.exp2(depth_now) * factor[first + half, g : g + 1, :]
                    total = down - up if total is None else (total + down) - up
                acc[8 + chunk * 8 : 16 + chunk * 8, lanes] = total
        for half in range(2):
            block = first + half
            lanes = slice(half * LANES, (half + 1) * LANES)
            acc[7:8, lanes] = edge[block, 0:1, :]
            acc[96:98, lanes] = edge[block, 1:3, :]
            keep = sun[0, block] == 1
            scale = jnp.where(keep, mu[pl.ds(block, 1), :], 0.0)
            heat[slot, pl.ds(2 * pair + half, LEVELS, stride=STEP), :] = (
                acc[7 : 7 + LEVELS, lanes] - acc[8 : 8 + LEVELS, lanes]
            ) * scale

    def body(s, _):
        base = s * (STEP * 2)
        for sub in range(2):
            for copy in fetch(s * 2 + sub):
                copy.wait()
        lit = sun[0, base]
        for block in range(1, STEP * 2):
            lit = lit | sun[0, base + block]

        @pl.when(lit != 0)
        def _():
            for sub in range(2):
                for pair in range(STEP // 2):
                    fluxes(base + sub * STEP, pair, (acc_a, acc_b)[pair % 2], s * 2 + sub)
                    if pair % 4 == 3:
                        flush(s * 2 + sub, pair // 4).start()

        @pl.when(lit == 0)
        def _():
            for sub in range(2):
                heat[s * 2 + sub] = jnp.zeros(heat.shape[1:], f32)
                for part in range(2):
                    flush(s * 2 + sub, part).start()

        return 0

    lax.fori_loop(0, steps // 2, body, 0)
    for s in range(steps):
        for part in range(2):
            flush(s, part).wait()


def finish_kernel(got, temp, capacity, conduct, soil_out):
    senders = got.shape[0] // 2
    values = got[pl.ds(0, senders, stride=2), :]
    ids = got[pl.ds(1, senders, stride=2), :]
    tiles = [(ids[8 * t : 8 * t + 8], values[8 * t : 8 * t + 8]) for t in range(senders // 8)]
    sums = []
    for block in range(soil_out.shape[1]):
        parts = [jnp.where(i == float(block), v, 0.0) for i, v in tiles]
        while len(parts) > 1:
            parts = [x + y for x, y in zip(parts[::2], parts[1::2])]
        sums.append(jnp.sum(parts[0], axis=0, keepdims=True))
    flux = jnp.concatenate(sums, axis=0)
    layers = temp.shape[0]
    ratio = []
    inverse = []
    for layer in range(layers):
        pivot = capacity[layer] + conduct[layer]
        if layer > 0:
            above = conduct[layer - 1]
            pivot = (pivot + above) + above * ratio[-1]
        inverse.append(1.0 / pivot)
        ratio.append(-conduct[layer] * inverse[-1])
    scaled = [(capacity[0] * temp[0] + flux) * inverse[0]]
    for layer in range(1, layers):
        right = capacity[layer] * temp[layer] + conduct[layer - 1] * scaled[-1]
        scaled.append(right * inverse[layer])
    solved = scaled[-1]
    soil_out[layers - 1] = solved
    for layer in range(layers - 2, -1, -1):
        solved = scaled[layer] - ratio[layer] * solved
        soil_out[layer] = solved


def surface_call(sun, owner, target, weight, absorption, path, cosine, albedo, area, cell, devices):
    blocks = path.shape[1]
    steps = blocks // STEP
    anywhere = pl.BlockSpec(memory_space=pl.ANY)
    shapes = [
        jax.ShapeDtypeStruct((blocks, KROWS, LANES), bf16),
        jax.ShapeDtypeStruct((blocks, GP, LANES), f32),
        jax.ShapeDtypeStruct((blocks, 8, LANES), f32),
        jax.ShapeDtypeStruct((GP, 256), f32),
        jax.ShapeDtypeStruct((devices, 2, LANES), f32),
    ]
    return pl.pallas_call(
        surface_kernel,
        in_specs=[anywhere] * 10,
        out_specs=[anywhere] * 5,
        out_shape=shapes,
        scratch_shapes=[
            pltpu.SMEM((1, blocks), jnp.int32),
            pltpu.SMEM((1, blocks), jnp.int32),
            pltpu.SMEM((1, blocks), jnp.int32),
            pltpu.SMEM((GP,), f32),
            pltpu.VMEM((GP, LEVELS), f32),
            pltpu.VMEM((steps, LEVELS, STEP, LANES), bf16),
            pltpu.VMEM((blocks, LANES), bf16),
            pltpu.VMEM((blocks, LANES), bf16),
            pltpu.VMEM((blocks, LANES), f32),
            pltpu.VMEM((blocks, LANES), jnp.int32),
        ]
        + [pltpu.VMEM(shape.shape, shape.dtype) for shape in shapes]
        + [
            pltpu.VMEM((2, KROWS * WIDE + 32, LANES), f32),
            pltpu.VMEM((GP, LANES), f32),
            pltpu.VMEM((blocks, LANES), f32),
            pltpu.SemaphoreType.DMA((9 + steps,)),
            pltpu.SemaphoreType.DMA((2 + 3 * steps,)),
        ],
        compiler_params=pltpu.CompilerParams(vmem_limit_bytes=60 * 1024 * 1024),
        cost_estimate=pl.CostEstimate(flops=10**9, bytes_accessed=4 * 10**6, transcendentals=10**6),
        name="surface",
    )(sun, owner, target, weight, absorption, path, cosine, albedo, area, cell)


def radiate_call(sun, coef, rows, factor, edge, cosine):
    blocks = rows.shape[0]
    anywhere = pl.BlockSpec(memory_space=pl.ANY)
    return pl.pallas_call(
        radiate_kernel,
        in_specs=[anywhere] * 6,
        out_specs=anywhere,
        out_shape=jax.ShapeDtypeStruct((LEVELS, blocks, LANES), f32),
        scratch_shapes=[
            pltpu.SMEM(sun.shape, jnp.int32),
            pltpu.VMEM(coef.shape, f32),
            pltpu.VMEM(cosine.shape, bf16),
            pltpu.VMEM((CHUNKS * GP * 8, 256), bf16),
            pltpu.VMEM(rows.shape, bf16),
            pltpu.VMEM(factor.shape, f32),
            pltpu.VMEM(edge.shape, f32),
            pltpu.VMEM((blocks, LANES), f32),
            pltpu.VMEM((blocks, LANES), f32),
            pltpu.VMEM((104, 256), f32),
            pltpu.VMEM((104, 256), f32),
            pltpu.VMEM((blocks // STEP, KROWS * STEP, LANES), f32),
            pltpu.SemaphoreType.DMA((4, max(blocks // STEP, 3))),
            pltpu.SemaphoreType.DMA((blocks // STEP, 2)),
        ],
        compiler_params=pltpu.CompilerParams(vmem_limit_bytes=60 * 1024 * 1024),
        cost_estimate=pl.CostEstimate(flops=10**10, bytes_accessed=6 * 10**6, transcendentals=24 * 10**6),
        name="radiate",
    )(sun, coef, rows, factor, edge, cosine)


def finish_call(got, temp, capacity, conduct):
    return pl.pallas_call(
        finish_kernel,
        out_shape=jax.ShapeDtypeStruct(temp.shape, f32),
        compiler_params=pltpu.CompilerParams(vmem_limit_bytes=4 * 1024 * 1024),
        name="finish",
    )(got.reshape(-1, LANES), temp, capacity, conduct)


def local(
    absorber, cos_zenith, albedo, absorption, gpoint_weight, sunlit, area_weight,
    land_owner, land_block, land_cell, soil_temp, heat_capacity, conductance,
):
    devices = lax.axis_size(("lon", "lat"))
    path = jnp.transpose(absorber, (1, 0, 2))
    sun = sunlit.T
    rows, factor, edge, coef, send = surface_call(
        sun, land_owner.T, land_block.T, gpoint_weight, absorption, path,
        cos_zenith, albedo, area_weight, land_cell, devices,
    )
    got = lax.all_to_all(send, ("lon", "lat"), 0, 0, tiled=True)
    heat = radiate_call(sun, coef, rows, factor, edge, cos_zenith)
    return jnp.transpose(heat, (1, 0, 2)), finish_call(got, soil_temp, heat_capacity, conductance)


def solution(mesh):
    columns = P("lat", "lon")
    land = P(None, ("lon", "lat"), None)
    in_specs = (
        P("lat", None, "lon"), columns, columns, P(), P(), columns, columns,
        columns, columns, columns, land, land, land,
    )
    out_specs = (P("lat", None, "lon"), land)
    return jax.shard_map(local, mesh=mesh, in_specs=in_specs, out_specs=out_specs, check_vma=False)
```
